128 devices in a mesh: dp: 16 (over y, x), tensor: 8 (over z, core).
Axes of the slice: x: 4, y: 4, z: 4, core: 2. Of those that a mesh axis runs over, the one named last changes fastest.
Arguments:
- gate_pre: bfloat16 [8192, 14336], P('dp', 'tensor'), may hold values from -6 to 6
- up_pre: bfloat16 [8192, 14336], P('dp', 'tensor'), may hold values from -6 to 6
- out_grad: bfloat16 [8192, 4096], P(('dp', 'tensor')), may hold values from -0.25 to 0.25
- q_start: float32 [8, 4096, 32], P('tensor'), may hold values from -6 to 6
Outputs:
- p_factor: float32 [14336, 32], P('tensor')
- q_factor: float32 [8, 4096, 32], P('tensor')
- new_error: bfloat16 [16, 14336, 4096], P('dp', 'tensor')
The draws below stay inside these ranges and needn't reach their ends.
All inputs are finite; a program needn't handle non-finite values.
Results may differ from the reference program's by a relative error of at most 0.017.
Values may be sent and summed in bfloat16 or wider, within the bound.
A program may use at most 128 MiB of HBM per device.

```python
import jax
import jax.numpy as jnp
from jax import lax

D = 4096
FF = 14336
RANK = 32
TOK_REP = 512
TOKENS = 8192
N_DP = 16
N_TENSOR = 8


def block_levels(stream_key, shape, shards, smallest, high):
    gain = 1.0
    for axis_at, parts in shards:
        draws = jax.random.uniform(jax.random.fold_in(jax.random.fold_in(stream_key, 6), axis_at), (parts,), jnp.float32, smallest / len(shards), high / len(shards))
        gain = gain * jnp.repeat(jnp.exp(draws), shape[axis_at] // parts).reshape((-1,) + (1,) * (len(shape) - 1 - axis_at))
    return gain


def noise(stream_key, shape, width, limit, cuts=(), kind=jnp.bfloat16):
    loudness = block_levels(stream_key, shape, cuts, -0.22, 0.18) if cuts else 1.0
    values = jax.random.normal(stream_key, shape, jnp.float32) * width * loudness
    return jnp.minimum(jnp.maximum(values, -limit), limit).astype(kind)


def setup_inputs(seed: int = 0) -> dict:
    key_list = jax.random.split(jax.random.key(seed), 5)
    return {
        "gate_pre": noise(key_list[0], (TOKENS, FF), 1.0, 6.0, ((0, 16), (1, 8))),
        "up_pre": noise(key_list[1], (TOKENS, FF), 1.0, 6.0, ((0, 16), (1, 8))),
        "out_grad": noise(key_list[2], (TOKENS, D), TOK_REP ** -0.5, 0.25, ((0, 128),)),
        "q_start": noise(key_list[3], (N_TENSOR, D, RANK), 1.0, 6.0, ((0, 8),), jnp.float32),
    }


epsilon = 1e-06
HIGH = lax.Precision.HIGHEST

def orthonormal(power):
    rank = power.shape[1]
    basis = jnp.zeros(power.shape, jnp.float32)
    for index in range(rank):
        column = power[:, index]
        projection = jnp.dot(basis.T, column, precision=HIGH)
        remainder = column - jnp.dot(basis, projection, precision=HIGH)
        scaled = remainder * lax.rsqrt(jnp.sum(remainder * remainder) + epsilon)
        basis = basis.at[:, index].set(scaled)
    return basis

def reference(gate_pre, up_pre, out_grad, q_start):
    hidden = (jax.nn.silu(gate_pre.astype(jnp.float32)) * up_pre.astype(jnp.float32)).astype(jnp.bfloat16)
    shard = FF // N_TENSOR
    hidden_split = hidden.reshape(N_DP, TOK_REP, N_TENSOR, shard).transpose(2, 0, 1, 3)
    grad_split = out_grad.reshape(N_DP, TOK_REP, D)
    grad_wide = grad_split.astype(jnp.float32)

    def one_shard(packed):
        hidden_part, q_old = packed
        hidden_wide = hidden_part.astype(jnp.float32)
        projected = jnp.einsum('ntd,dr->ntr', grad_wide, q_old, precision=HIGH)
        power = jnp.einsum('ntf,ntr->fr', hidden_wide, projected, precision=HIGH)
        basis = orthonormal(power)
        mapped = jnp.einsum('ntf,fr->ntr', hidden_wide, basis, precision=HIGH)
        q_mean = jnp.einsum('ntd,ntr->dr', grad_wide, mapped, precision=HIGH) / N_DP

        def one_error(pair):
            rows, grads = pair
            full = jnp.dot(rows.T, grads, preferred_element_type=jnp.float32)
            return (full - jnp.dot(basis, q_mean.T, precision=HIGH)).astype(jnp.bfloat16)
        errors = lax.map(one_error, (hidden_part, grad_split))
        return (basis, q_mean, errors)
    bases, q_means, errors = lax.map(one_shard, (hidden_split, q_start))
    p_factor = bases.reshape(FF, RANK)
    new_error = errors.transpose(1, 0, 2, 3).reshape(N_DP, FF, D)
    return (p_factor, q_means, new_error)
```

```python
import functools

import jax
import jax.numpy as jnp
from jax import lax
from jax.experimental import pallas as pl
from jax.experimental.pallas import tpu as pltpu
from jax.sharding import PartitionSpec as P

EPSILON = 1e-06
HIGH = lax.Precision.HIGHEST
BF16 = jnp.bfloat16
F32 = jnp.float32
MESH = pl.DeviceIdType.MESH

TOK = 512
ROWS = 64
D = 4096
FF = 1792
RANK = 32
CHUNKS = 8
WIDTH = D // CHUNKS
DP = 16
AHEAD = 3
PSLICE = 128
PSLICES = FF // PSLICE
QSLICE = D // DP
TILE = 256


def dot(a, b, contract):
    return lax.dot_general(a, b, ((contract[:1], contract[1:]), ((), ())), preferred_element_type=F32)


def split2(x):
    high = x.astype(BF16)
    low = (x - high.astype(F32)).astype(BF16)
    return jnp.concatenate([high, low], axis=0)


def join2(x):
    return x[:RANK] + x[RANK:]


def gram_schmidt(gram, coeff_ref):
    y = gram
    rows = lax.broadcasted_iota(jnp.int32, (RANK, RANK), 0)
    cols = lax.broadcasted_iota(jnp.int32, (RANK, RANK), 1)
    u = jnp.where(rows == cols, 1.0, 0.0).astype(F32)
    for j in range(RANK):
        y_row = y[j : j + 1, :]
        u_row = u[j : j + 1, :]
        norm = jnp.sum(y_row * u_row, axis=1, keepdims=True)
        scale = lax.rsqrt(jnp.maximum(norm, 0.0) + EPSILON)
        coeff_ref[j : j + 1, :] = u_row * scale
        if j < RANK - 1:
            factor = y[:, j : j + 1] * (scale * scale)
            y = y - factor * y_row
            u = u - factor * u_row


def exchange_kernel(
    gate_hbm, up_hbm, out_grad_hbm, q_hbm,
    grad_ref, p_ref, q_ref,
    g_buf, gate_buf, up_buf, h_buf, ht_buf, q_buf, qs_buf, proj, coeff,
    p_part, p_in, p_all, q_part, q_in, q_all,
    local_sem, sem_up_s, sem_up_r, sem_dn_s, sem_dn_r, sem_fu_s, sem_fu_r, sem_fd_s, sem_fd_r,
    sem_sib_s, sem_sib_r, sem_ar_s, sem_ar_r,
):
    dp = lax.axis_index("dp")
    tensor = lax.axis_index("tensor")
    z = tensor // 2
    core = tensor % 2
    t_up = lax.rem(z + 1, 4) * 2 + core
    t_dn = lax.rem(z + 3, 4) * 2 + core
    t_far = lax.rem(z + 2, 4) * 2 + core
    t_sib = z * 2 + 1 - core

    def rows_of(t):
        return pl.ds(pl.multiple_of(t * ROWS, ROWS), ROWS)

    def local_g(c):
        return pltpu.make_async_copy(
            out_grad_hbm.at[:, pl.ds(pl.multiple_of(c * WIDTH, WIDTH), WIDTH)],
            g_buf.at[c, rows_of(tensor), :], local_sem.at[c])

    def local_in(k):
        src, dst = ((gate_hbm, gate_buf), (up_hbm, up_buf), (q_hbm, q_buf))[k]
        return pltpu.make_async_copy(src, dst, local_sem.at[CHUNKS + k])

    for c in range(CHUNKS):
        local_g(c).start()
    for k in range(3):
        local_in(k).start()

    barrier = pltpu.get_barrier_semaphore()
    for t in (t_up, t_dn, t_sib):
        pl.semaphore_signal(barrier, inc=1, device_id={"tensor": t}, device_id_type=MESH)

    def greet(k, carry):
        pl.semaphore_signal(
            barrier, inc=1, device_id={"dp": lax.rem(dp + k, DP)}, device_id_type=MESH)
        return carry

    lax.fori_loop(1, DP, greet, 0)
    pl.semaphore_wait(barrier, 3 + DP - 1)

    def remote(c, rows, t, send, recv):
        ref = g_buf.at[c, rows, :]
        return pltpu.make_async_remote_copy(
            src_ref=ref, dst_ref=ref, send_sem=send, recv_sem=recv,
            device_id={"tensor": t}, device_id_type=MESH)

    half = ROWS // 2

    def first_half(t):
        return pl.ds(pl.multiple_of(t * ROWS, half), half)

    def last_half(t):
        return pl.ds(pl.multiple_of(t * ROWS + half, half), half)

    def send_up(c):
        return remote(c, rows_of(tensor), t_up, sem_up_s.at[c], sem_up_r.at[c])

    def send_dn(c):
        return remote(c, rows_of(tensor), t_dn, sem_dn_s.at[c], sem_dn_r.at[c])

    def forward_up(c):
        return remote(c, first_half(t_dn), t_up, sem_fu_s.at[c], sem_fu_r.at[c])

    def forward_dn(c):
        return remote(c, last_half(t_up), t_dn, sem_fd_s.at[c], sem_fd_r.at[c])

    def send_sib(c, t, k):
        return remote(c, rows_of(t), t_sib, sem_sib_s.at[c, k], sem_sib_r.at[c, k])

    def start_own(c):
        local_g(c).wait()
        send_up(c).start()
        send_dn(c).start()
        send_sib(c, tensor, 0).start()

    def middle(c):
        remote(c, rows_of(t_dn), t_up, sem_up_s.at[c], sem_up_r.at[c]).wait_recv()
        forward_up(c).start()
        send_sib(c, t_dn, 1).start()
        remote(c, rows_of(t_up), t_dn, sem_dn_s.at[c], sem_dn_r.at[c]).wait_recv()
        forward_dn(c).start()
        send_sib(c, t_up, 2).start()

    def last(c):
        remote(c, first_half(t_far), t_up, sem_fu_s.at[c], sem_fu_r.at[c]).wait_recv()
        remote(c, last_half(t_far), t_dn, sem_fd_s.at[c], sem_fd_r.at[c]).wait_recv()
        send_sib(c, t_far, 3).start()

    def arrived(c):
        for k in range(4):
            send_sib(c, tensor, k).wait_recv()

    for c in range(AHEAD):
        start_own(c)

    local_in(0).wait()
    local_in(1).wait()

    def make_hidden(i, carry):
        rows = pl.ds(pl.multiple_of(i * 64, 64), 64)
        v = gate_buf[rows, :].astype(F32)
        w = up_buf[rows, :].astype(F32)
        h_buf[rows, :] = ((0.5 * v) * (1.0 + jnp.tanh(0.5 * v)) * w).astype(BF16)
        return carry

    lax.fori_loop(0, TOK // 64, make_hidden, 0)

    def turn_hidden(i, carry):
        cols = pl.ds(pl.multiple_of(i * TILE, TILE), TILE)
        ht_buf[cols, :] = h_buf[:, cols].T
        return carry

    lax.fori_loop(0, FF // TILE, turn_hidden, 0)
    local_in(2).wait()
    qs_buf[...] = split2(q_buf[...])
    proj[...] = jnp.zeros_like(proj)

    def gather_step(i, carry):
        @pl.when(i + AHEAD < CHUNKS)
        def _():
            start_own(i + AHEAD)

        @pl.when(i < CHUNKS)
        def _():
            middle(i)

        @pl.when(jnp.logical_and(i >= 1, i <= CHUNKS))
        def _():
            last(i - 1)

        @pl.when(i >= 2)
        def _():
            c = i - 2
            arrived(c)
            cols = pl.ds(pl.multiple_of(c * WIDTH, WIDTH), WIDTH)
            proj[...] += dot(qs_buf[:, cols], g_buf[c], (1, 1))

            def grad_tile(m, carry):
                rows = pl.ds(pl.multiple_of(m * TILE, TILE), TILE)
                grad_ref[rows, cols] = dot(ht_buf[rows, :], g_buf[c], (1, 0))
                return carry

            lax.fori_loop(0, FF // TILE, grad_tile, 0)

        return carry

    lax.fori_loop(0, CHUNKS + 2, gather_step, 0)

    projected = split2(join2(proj[...]))
    power = join2(dot(projected, h_buf[...], (1, 0)))
    for s in range(DP):
        if s < PSLICES:
            p_part[s] = power[:, s * PSLICE : (s + 1) * PSLICE]
        else:
            p_part[s] = jnp.zeros((RANK, PSLICE), F32)

    def all_reduce(part, landing, total, sums, k0):
        def scatter(k):
            peer = lax.rem(dp + k, DP)
            return pltpu.make_async_remote_copy(
                src_ref=part.at[peer], dst_ref=landing.at[dp],
                send_sem=sem_ar_s.at[k0], recv_sem=sem_ar_r.at[k0],
                device_id={"dp": peer}, device_id_type=MESH)

        def gather(k):
            peer = lax.rem(dp + k, DP)
            return pltpu.make_async_remote_copy(
                src_ref=total.at[dp], dst_ref=total.at[dp],
                send_sem=sem_ar_s.at[k0 + 1], recv_sem=sem_ar_r.at[k0 + 1],
                device_id={"dp": peer}, device_id_type=MESH)

        def start(copy):
            def body(k, carry):
                copy(k).start()
                return carry

            lax.fori_loop(1, DP, body, 0)

        def wait_all(ref, sem):
            pltpu.make_async_copy(ref.at[pl.ds(0, DP - 1)], ref.at[pl.ds(0, DP - 1)], sem).wait()

        start(scatter)
        landing[dp] = part[dp]
        wait_all(landing, sem_ar_r.at[k0])
        total[dp] = sums(landing)
        start(gather)
        wait_all(total, sem_ar_r.at[k0 + 1])
        wait_all(part, sem_ar_s.at[k0])
        wait_all(total, sem_ar_s.at[k0 + 1])

    def sum_p(landing):
        value = landing[0]
        for s in range(1, DP):
            value = value + landing[s]
        return value

    def sum_q(landing):
        value = landing[0].astype(F32)
        for s in range(1, DP):
            value = value + landing[s].astype(F32)
        return (value * (1.0 / DP)).astype(BF16)

    all_reduce(p_part, p_in, p_all, sum_p, 0)
    power = jnp.concatenate([p_all[s] for s in range(PSLICES)], axis=1)
    gram = lax.dot_general(
        power, power, (((1,), (1,)), ((), ())), precision=HIGH, preferred_element_type=F32)
    gram_schmidt(gram, coeff)
    basis = jnp.dot(coeff[...], power, precision=HIGH, preferred_element_type=F32)
    p_ref[...] = basis

    mapped = split2(join2(dot(split2(basis), ht_buf[...], (1, 0))))
    for c in range(CHUNKS):
        terms = join2(dot(mapped, g_buf[c], (1, 0))).astype(BF16)
        for k in range(WIDTH // QSLICE):
            q_part[c * (WIDTH // QSLICE) + k] = terms[:, k * QSLICE : (k + 1) * QSLICE]
    all_reduce(q_part, q_in, q_all, sum_q, 2)
    for s in range(DP):
        q_ref[:, s * QSLICE : (s + 1) * QSLICE] = q_all[s].astype(F32)

    def drain(c, carry):
        send_up(c).wait_send()
        send_dn(c).wait_send()
        forward_up(c).wait_send()
        forward_dn(c).wait_send()
        for k in range(4):
            send_sib(c, tensor, k).wait_send()
        return carry

    lax.fori_loop(0, CHUNKS, drain, 0)


ROW_TILE = 128


def error_kernel(grad_ref, p_ref, q_ref, p_out, q_out, error_ref, q2):
    step = pl.program_id(0)

    @pl.when(step == 0)
    def _():
        p_out[...] = p_ref[...]
        q_out[...] = q_ref[...]
        q_once = q_ref[...].astype(BF16)
        q2[...] = jnp.concatenate([q_once, q_once], axis=0)

    rows = pl.ds(pl.multiple_of(step * ROW_TILE, ROW_TILE), ROW_TILE)
    p2 = split2(p_ref[:, rows])
    for k in range(4):
        cols = pl.ds(k * (D // 4), D // 4)
        low_rank = dot(p2, q2[:, cols], (0, 0))
        error_ref[:, cols] = (grad_ref[rows, cols] - low_rank).astype(BF16)


def on_device(gate_pre, up_pre, out_grad, q_start):
    q_turned = q_start[0].T
    any_space = pl.BlockSpec(memory_space=pl.ANY)
    vmem_space = pl.BlockSpec(memory_space=pltpu.VMEM)
    dma = pltpu.SemaphoreType.DMA
    grad, p_turned, q_mean = pl.pallas_call(
        exchange_kernel,
        out_shape=(
            pltpu.VMEM((FF, D), F32),
            pltpu.VMEM((RANK, FF), F32),
            pltpu.VMEM((RANK, D), F32),
        ),
        in_specs=[any_space] * 4,
        out_specs=(vmem_space,) * 3,
        scratch_shapes=[
            pltpu.VMEM((CHUNKS, TOK, WIDTH), BF16),
            pltpu.VMEM((TOK, FF), BF16),
            pltpu.VMEM((TOK, FF), BF16),
            pltpu.VMEM((TOK, FF), BF16),
            pltpu.VMEM((FF, TOK), BF16),
            pltpu.VMEM((RANK, D), F32),
            pltpu.VMEM((2 * RANK, D), BF16),
            pltpu.VMEM((2 * RANK, TOK), F32),
            pltpu.VMEM((RANK, RANK), F32),
            pltpu.VMEM((DP, RANK, PSLICE), F32),
            pltpu.VMEM((DP, RANK, PSLICE), F32),
            pltpu.VMEM((DP, RANK, PSLICE), F32),
            pltpu.VMEM((DP, RANK, QSLICE), BF16),
            pltpu.VMEM((DP, RANK, QSLICE), BF16),
            pltpu.VMEM((DP, RANK, QSLICE), BF16),
            dma((CHUNKS + 3,)),
            dma((CHUNKS,)), dma((CHUNKS,)), dma((CHUNKS,)), dma((CHUNKS,)),
            dma((CHUNKS,)), dma((CHUNKS,)), dma((CHUNKS,)), dma((CHUNKS,)),
            dma((CHUNKS, 4)), dma((CHUNKS, 4)), dma((4,)), dma((4,)),
        ],
        compiler_params=pltpu.CompilerParams(
            collective_id=0, has_side_effects=True, vmem_limit_bytes=24 * 2**20),
        name="exchange",
    )(*[pltpu.with_memory_space_constraint(v, pltpu.HBM) for v in (gate_pre, up_pre, out_grad, q_turned)])
    p_out, q_out, new_error = pl.pallas_call(
        error_kernel,
        grid=(FF // ROW_TILE,),
        out_shape=(
            jax.ShapeDtypeStruct((RANK, FF), F32),
            jax.ShapeDtypeStruct((RANK, D), F32),
            jax.ShapeDtypeStruct((FF, D), BF16),
        ),
        in_specs=[vmem_space] * 3,
        out_specs=(
            pl.BlockSpec((RANK, FF), lambda i: (0, 0)),
            pl.BlockSpec((RANK, D), lambda i: (0, 0)),
            pl.BlockSpec((ROW_TILE, D), lambda i: (i, 0)),
        ),
        scratch_shapes=[pltpu.VMEM((2 * RANK, D), BF16)],
        compiler_params=pltpu.CompilerParams(vmem_limit_bytes=24 * 2**20),
        name="error",
    )(grad, p_turned, q_mean)
    return (p_out.T, q_out.T[None], new_error[None])


def solution(mesh):
    placed = (
        P("dp", "tensor"),
        P("dp", "tensor"),
        P(("dp", "tensor"), None),
        P("tensor", None, None),
    )
    return jax.shard_map(
        on_device,
        mesh=mesh,
        in_specs=placed,
        out_specs=(P("tensor", None), P("tensor", None, None), P("dp", "tensor", None)),
        check_vma=False,
    )
```

```python
import functools

import jax
import jax.numpy as jnp
from jax import lax
from jax.experimental import pallas as pl
from jax.experimental.pallas import tpu as pltpu
from jax.sharding import PartitionSpec as P

EPSILON = 1e-06
HIGH = lax.Precision.HIGHEST
BF16 = jnp.bfloat16
F32 = jnp.float32
MESH = pl.DeviceIdType.MESH

TOK = 512
ROWS = 64
D = 4096
FF = 1792
RANK = 32
HALF = ROWS // 2
CHIP = 2 * ROWS
DP = 16
PSLICE = 128
PSLICES = FF // PSLICE
QSLICE = D // DP
TILE = 256
WIDTH = 512
GRAD_TILE = 448
BLOCK = 4
ERROR_TILE = 128
ERROR_WIDTH = 256
VMEM_BYTES = 24 * 2**20


def dot(a, b, contract):
    return lax.dot_general(a, b, ((contract[:1], contract[1:]), ((), ())), preferred_element_type=F32)


def split2(x):
    high = x.astype(BF16)
    low = (x - high.astype(F32)).astype(BF16)
    return jnp.concatenate([high, low], axis=0)


def join2(x):
    return x[:RANK] + x[RANK:]


def gram_schmidt(gram, coeff_ref):
    rows = lax.broadcasted_iota(jnp.int32, (RANK, RANK), 0)
    cols = lax.broadcasted_iota(jnp.int32, (RANK, RANK), 1)
    y = gram
    u = jnp.where(rows == cols, 1.0, 0.0).astype(F32)
    base = 0

    def spread_row(m, r):
        return jnp.broadcast_to(m[r : r + 1, :], (8, RANK))

    def tall(m, n):
        return jnp.concatenate([m] * (n // 8), axis=0) if n > 8 else m

    for j in range(0, RANK, BLOCK):
        at = j - base
        left = RANK - base
        y_row = [spread_row(y, at + a) for a in range(BLOCK)]
        u_row = [spread_row(u, at + a) for a in range(BLOCK)]
        y_col = [jnp.broadcast_to(y[:, j + a : j + a + 1], (left, RANK)) for a in range(BLOCK)]
        pairs = [(a, c) for a in range(BLOCK) for c in range(a, BLOCK)]
        x = {
            (a, c): jnp.broadcast_to(
                jnp.sum(u_row[a] * y_row[c], axis=1, keepdims=True), (8, RANK))
            for a, c in pairs
        }
        v = {(a, c): spread_row(y_col[a], at + c) for a, c in pairs if c > a}
        inverse = []
        for a in range(BLOCK):
            norm = x[a, a]
            scale = lax.rsqrt(jnp.maximum(norm, 0.0) + EPSILON)
            inverse.append(scale * scale)
            coeff_ref[j + a : j + a + 1, :] = (u_row[a] * scale)[:1]
            f = {c: v[a, c] * inverse[a] for c in range(a + 1, BLOCK)}
            for c in range(a + 1, BLOCK):
                for d in range(c, BLOCK):
                    x[c, d] = x[c, d] - f[c] * x[a, d] - f[d] * (x[a, c] - norm * f[c])
                    if d > c:
                        v[c, d] = v[c, d] - f[c] * v[a, d]
                y_row[c] = y_row[c] - f[c] * y_row[a]
                u_row[c] = u_row[c] - f[c] * u_row[a]
                y_col[c] = y_col[c] - tall(f[c], left) * y_col[a]
        if j + BLOCK < RANK:
            for a in range(BLOCK):
                y = y - y_col[a] * tall(inverse[a] * y_row[a], left)
                u = u - y_col[a] * tall(inverse[a] * u_row[a], left)
            if (j + BLOCK) % 8 == 0:
                y = y[j + BLOCK - base :, :]
                u = u[j + BLOCK - base :, :]
                base = j + BLOCK


def exchange_kernel(
    gate_hbm, up_hbm, out_grad_hbm, q_hbm,
    grad_ref, p_ref, q_ref, p_turned_ref,
    g_buf, gate_buf, up_buf, h_buf, ht_buf, q_buf, qs_buf, proj, coeff,
    p_part, p_in, p_all, q_part, q_in, q_all,
    local_sem, own_s, own_r, far_s, far_r, sib_s, sib_r, sum_s, sum_r,
):
    dp = lax.axis_index("dp")
    tensor = lax.axis_index("tensor")
    z = tensor // 2
    core = lax.rem(tensor, 2)
    z_up, z_far, z_dn = lax.rem(z + 1, 4), lax.rem(z + 2, 4), lax.rem(z + 3, 4)
    t_up, t_far, t_dn = z_up * 2 + core, z_far * 2 + core, z_dn * 2 + core
    t_sib = z * 2 + 1 - core
    y = dp // 4
    x = lax.rem(dp, 4)
    offsets = sorted(
        ((a, b) for a in range(4) for b in range(4) if a or b),
        key=lambda o: -(min(o[0], 4 - o[0]) + min(o[1], 4 - o[1])),
    )
    peers = [lax.rem(y + a, 4) * 4 + lax.rem(x + b, 4) for a, b in offsets]

    def half_of(t, h):
        return pl.ds(pl.multiple_of(t * ROWS + h * HALF, HALF), HALF)

    def local_g(h):
        return pltpu.make_async_copy(
            out_grad_hbm.at[pl.ds(h * HALF, HALF), :], g_buf.at[half_of(tensor, h), :],
            local_sem.at[h])

    def local_in(k):
        src, dst = ((gate_hbm, gate_buf), (up_hbm, up_buf), (q_hbm, q_buf))[k]
        return pltpu.make_async_copy(src, dst, local_sem.at[2 + k])

    barrier = pltpu.get_barrier_semaphore()
    for t in (t_up, t_dn, t_sib):
        pl.semaphore_signal(barrier, inc=1, device_id={"tensor": t}, device_id_type=MESH)
    for peer in peers:
        pl.semaphore_signal(barrier, inc=1, device_id={"dp": peer}, device_id_type=MESH)
    for h in range(2):
        local_g(h).start()
    for k in range(3):
        local_in(k).start()
    pl.semaphore_wait(barrier, 3 + DP - 1)

    def piece(t, h, to, send, recv):
        ref = g_buf.at[half_of(t, h), :]
        return pltpu.make_async_remote_copy(
            src_ref=ref, dst_ref=ref, send_sem=send, recv_sem=recv,
            device_id={"tensor": to}, device_id_type=MESH)

    def own(way, k):
        h = k if way == 0 else 1 - k
        return piece(tensor, h, (t_up, t_dn)[way], own_s.at[way, k], own_r.at[way, k])

    def onward(way):
        return piece((t_dn, t_up)[way], way, (t_up, t_dn)[way], far_s.at[way], far_r.at[way])

    def across(n, t, h):
        return piece(t, h, t_sib, sib_s.at[n], sib_r.at[n])

    for h in range(2):
        local_g(h).wait()
    for k in range(2):
        for way in range(2):
            own(way, k).start()
    for h in range(2):
        across(h, tensor, h).start()

    local_in(0).wait()
    local_in(1).wait()

    def make_hidden(i, carry):
        rows = pl.ds(pl.multiple_of(i * 64, 64), 64)
        v = gate_buf[rows, :].astype(F32)
        w = up_buf[rows, :].astype(F32)
        h_buf[rows, :] = ((0.5 * v) * (1.0 + jnp.tanh(0.5 * v)) * w).astype(BF16)
        return carry

    lax.fori_loop(0, TOK // 64, make_hidden, 0)

    def turn_hidden(i, carry):
        cols = pl.ds(pl.multiple_of(i * TILE, TILE), TILE)
        ht_buf[cols, :] = h_buf[:, cols].T
        return carry

    lax.fori_loop(0, FF // TILE, turn_hidden, 0)
    local_in(2).wait()
    qs_buf[...] = split2(q_buf[...])

    def project(chip):
        rows = pl.ds(pl.multiple_of(chip * CHIP, CHIP), CHIP)
        proj[:, rows] = dot(qs_buf[...], g_buf[rows, :], (1, 1))

    def crossed(n):
        across(n, tensor, 0).wait_recv()

    crossed(0)
    crossed(1)
    project(z)
    for k in range(2):
        for way in range(2):
            own(way, k).wait_recv()
            if k == 0:
                onward(way).start()
            across(2 + 2 * k + way, (t_dn, t_up)[way], k if way == 0 else 1 - k).start()
    for n in range(2, 6):
        crossed(n)
    project(z_dn)
    project(z_up)
    for way in range(2):
        onward(way).wait_recv()
        across(6 + way, t_far, way).start()
    crossed(6)
    crossed(7)
    project(z_far)

    def grad_tiles(first, last):
        def body(m, carry):
            rows = pl.ds(pl.multiple_of(m * GRAD_TILE, GRAD_TILE), GRAD_TILE)
            for c in range(0, D, WIDTH):
                cols = pl.ds(c, WIDTH)
                grad_ref[rows, cols] = dot(ht_buf[rows, :], g_buf[:, cols], (1, 0))
            return carry

        lax.fori_loop(first, last, body, 0)

    def scatter(part, landing, peer, n):
        return pltpu.make_async_remote_copy(
            src_ref=part.at[peer], dst_ref=landing.at[dp], send_sem=sum_s.at[n],
            recv_sem=sum_r.at[n], device_id={"dp": peer}, device_id_type=MESH)

    def gather(total, peer, n):
        return pltpu.make_async_remote_copy(
            src_ref=total.at[dp], dst_ref=total.at[dp], send_sem=sum_s.at[n],
            recv_sem=sum_r.at[n], device_id={"dp": peer}, device_id_type=MESH)

    def wait_all(ref, sem):
        ref = ref.at[pl.ds(0, DP - 1)]
        pltpu.make_async_copy(ref, ref, sem).wait()

    power = join2(dot(split2(join2(proj[...])), h_buf[...], (1, 0)))
    for s in range(DP):
        if s < PSLICES:
            p_part[s] = power[:, s * PSLICE : (s + 1) * PSLICE]
        else:
            p_part[s] = jnp.zeros((RANK, PSLICE), F32)
    for peer in peers:
        scatter(p_part, p_in, peer, 0).start()
    p_in[dp] = p_part[dp]
    grad_tiles(0, FF // GRAD_TILE // 2)
    wait_all(p_in, sum_r.at[0])
    value = p_in[0]
    for s in range(1, DP):
        value = value + p_in[s]
    p_all[dp] = value
    for peer in peers:
        gather(p_all, peer, 1).start()
    grad_tiles(FF // GRAD_TILE // 2, FF // GRAD_TILE)
    wait_all(p_all, sum_r.at[1])

    power = jnp.concatenate([p_all[s] for s in range(PSLICES)], axis=1)
    gram = lax.dot_general(
        power, power, (((1,), (1,)), ((), ())), precision=HIGH, preferred_element_type=F32)
    gram_schmidt(gram, coeff)
    basis = jnp.dot(coeff[...], power, precision=HIGH, preferred_element_type=F32)
    p_ref[...] = basis

    basis2 = split2(basis)
    mapped = split2(join2(dot(basis2, ht_buf[...], (1, 0))))
    for c in range(0, D, WIDTH):
        terms = join2(dot(mapped, g_buf[:, c : c + WIDTH], (1, 0))).astype(BF16)
        for k in range(WIDTH // QSLICE):
            q_part[c // QSLICE + k] = terms[:, k * QSLICE : (k + 1) * QSLICE]
    for peer in peers:
        scatter(q_part, q_in, peer, 2).start()
    q_in[dp] = q_part[dp]
    p_turned_ref[...] = split2(p_ref[...]).T
    wait_all(q_in, sum_r.at[2])
    value = q_in[0].astype(F32)
    for s in range(1, DP):
        value = value + q_in[s].astype(F32)
    q_all[dp] = (value * (1.0 / DP)).astype(BF16)
    for peer in peers:
        gather(q_all, peer, 3).start()

    for way in range(2):
        for k in range(2):
            own(way, k).wait_send()
        onward(way).wait_send()
    for n in range(8):
        across(n, tensor, 0).wait_send()
    wait_all(p_part, sum_s.at[0])
    wait_all(p_all, sum_s.at[1])
    wait_all(q_part, sum_s.at[2])
    wait_all(q_all, sum_r.at[3])
    for s in range(DP):
        q_ref[:, s * QSLICE : (s + 1) * QSLICE] = q_all[s].astype(F32)
    wait_all(q_all, sum_s.at[3])


def error_kernel(
    grad_ref, p_ref, q_ref, p_turned_ref, p_out, q_out, error_out, q2, error_buf, sem, factor_sem
):
    factors = (
        pltpu.make_async_copy(p_ref, p_out, factor_sem.at[0]),
        pltpu.make_async_copy(q_ref, q_out, factor_sem.at[1]),
    )
    q_once = q_ref[...].astype(BF16)
    q2[...] = jnp.concatenate([q_once, q_once], axis=0)
    copies = []
    for m in range(FF // ERROR_TILE):
        rows = pl.ds(m * ERROR_TILE, ERROR_TILE)
        for c in range(0, D, ERROR_WIDTH):
            cols = pl.ds(c, ERROR_WIDTH)
            low_rank = dot(p_turned_ref[rows, :], q2[:, cols], (1, 0))
            error_buf[rows, cols] = (grad_ref[rows, cols] - low_rank).astype(BF16)
        copies.append(
            pltpu.make_async_copy(error_buf.at[rows], error_out.at[rows], sem.at[m]))
        copies[-1].start()
        if m == 0:
            for copy in factors:
                copy.start()
    for copy in copies:
        copy.wait()
    for copy in factors:
        copy.wait()


def on_device(gate_pre, up_pre, out_grad, q_start):
    hbm_in = [
        pltpu.with_memory_space_constraint(v, pltpu.HBM)
        for v in (gate_pre, up_pre, out_grad, q_start[0].T)
    ]
    any_space = pl.BlockSpec(memory_space=pl.ANY)
    vmem_space = pl.BlockSpec(memory_space=pltpu.VMEM)
    dma = pltpu.SemaphoreType.DMA
    grad, p_factor, q_factor, p_turned = pl.pallas_call(
        exchange_kernel,
        out_shape=(
            pltpu.VMEM((FF, D), F32),
            pltpu.VMEM((RANK, FF), F32),
            pltpu.VMEM((RANK, D), F32),
            pltpu.VMEM((FF, 2 * RANK), BF16),
        ),
        in_specs=[any_space] * 4,
        out_specs=(vmem_space,) * 4,
        scratch_shapes=[
            pltpu.VMEM((TOK, D), BF16),
            pltpu.VMEM((TOK, FF), BF16),
            pltpu.VMEM((TOK, FF), BF16),
            pltpu.VMEM((TOK, FF), BF16),
            pltpu.VMEM((FF, TOK), BF16),
            pltpu.VMEM((RANK, D), F32),
            pltpu.VMEM((2 * RANK, D), BF16),
            pltpu.VMEM((2 * RANK, TOK), F32),
            pltpu.VMEM((RANK, RANK), F32),
            pltpu.VMEM((DP, RANK, PSLICE), F32),
            pltpu.VMEM((DP, RANK, PSLICE), F32),
            pltpu.VMEM((DP, RANK, PSLICE), F32),
            pltpu.VMEM((DP, RANK, QSLICE), BF16),
            pltpu.VMEM((DP, RANK, QSLICE), BF16),
            pltpu.VMEM((DP, RANK, QSLICE), BF16),
            dma((5,)),
            dma((2, 2)), dma((2, 2)), dma((2,)), dma((2,)),
            dma((8,)), dma((8,)), dma((4,)), dma((4,)),
        ],
        compiler_params=pltpu.CompilerParams(
            collective_id=0, has_side_effects=True, vmem_limit_bytes=VMEM_BYTES),
        name="exchange",
    )(*hbm_in)
    p_out, q_out, new_error = pl.pallas_call(
        error_kernel,
        out_shape=(
            jax.ShapeDtypeStruct((RANK, FF), F32),
            jax.ShapeDtypeStruct((RANK, D), F32),
            jax.ShapeDtypeStruct((FF, D), BF16),
        ),
        in_specs=[vmem_space] * 4,
        out_specs=(any_space,) * 3,
        scratch_shapes=[
            pltpu.VMEM((2 * RANK, D), BF16),
            pltpu.VMEM((FF, D), BF16),
            dma((FF // ERROR_TILE,)),
            dma((2,)),
        ],
        compiler_params=pltpu.CompilerParams(vmem_limit_bytes=VMEM_BYTES),
        name="error",
    )(grad, p_factor, q_factor, p_turned)
    return (p_out.T, q_out.T[None], new_error[None])


def solution(mesh):
    placed = (
        P("dp", "tensor"),
        P("dp", "tensor"),
        P(("dp", "tensor"), None),
        P("tensor", None, None),
    )
    return jax.shard_map(
        on_device,
        mesh=mesh,
        in_specs=placed,
        out_specs=(P("tensor", None), P("tensor", None, None), P("dp", "tensor", None)),
        check_vma=False,
    )
```

```python
import functools

import jax
import jax.numpy as jnp
from jax import lax
from jax.experimental import pallas as pl
from jax.experimental.pallas import tpu as pltpu
from jax.sharding import PartitionSpec as P

EPSILON = 1e-06
HIGH = lax.Precision.HIGHEST
BF16 = jnp.bfloat16
F32 = jnp.float32
MESH = pl.DeviceIdType.MESH

TOK = 512
ROWS = 64
D = 4096
FF = 1792
RANK = 32
HALF = ROWS // 2
CHIP = 2 * ROWS
DP = 16
PSLICE = 128
PSLICES = FF // PSLICE
QSLICE = D // DP
TILE = 256
WIDTH = 512
GRAD_TILE = 448
BLOCK = 4
ERROR_TILE = 128
ERROR_WIDTH = 256
VMEM_BYTES = 24 * 2**20


def dot(a, b, contract):
    return lax.dot_general(a, b, ((contract[:1], contract[1:]), ((), ())), preferred_element_type=F32)


def split2(x):
    high = x.astype(BF16)
    low = (x - high.astype(F32)).astype(BF16)
    return jnp.concatenate([high, low], axis=0)


def join2(x):
    return x[:RANK] + x[RANK:]


def gram_schmidt(gram, coeff_ref):
    rows = lax.broadcasted_iota(jnp.int32, (RANK, RANK), 0)
    cols = lax.broadcasted_iota(jnp.int32, (RANK, RANK), 1)
    y = gram
    u = jnp.where(rows == cols, 1.0, 0.0).astype(F32)
    base = 0

    def spread_row(m, r):
        return jnp.broadcast_to(m[r : r + 1, :], (8, RANK))

    def tall(m, n):
        return jnp.concatenate([m] * (n // 8), axis=0) if n > 8 else m

    for j in range(0, RANK, BLOCK):
        at = j - base
        left = RANK - base
        y_row = [spread_row(y, at + a) for a in range(BLOCK)]
        u_row = [spread_row(u, at + a) for a in range(BLOCK)]
        y_col = [jnp.broadcast_to(y[:, j + a : j + a + 1], (left, RANK)) for a in range(BLOCK)]
        pairs = [(a, c) for a in range(BLOCK) for c in range(a, BLOCK)]
        x = {
            (a, c): jnp.broadcast_to(
                jnp.sum(u_row[a] * y_row[c], axis=1, keepdims=True), (8, RANK))
            for a, c in pairs
        }
        v = {(a, c): spread_row(y_col[a], at + c) for a, c in pairs if c > a}
        inverse = []
        for a in range(BLOCK):
            norm = x[a, a]
            scale = lax.rsqrt(jnp.maximum(norm, 0.0) + EPSILON)
            inverse.append(scale * scale)
            coeff_ref[j + a : j + a + 1, :] = (u_row[a] * scale)[:1]
            f = {c: v[a, c] * inverse[a] for c in range(a + 1, BLOCK)}
            for c in range(a + 1, BLOCK):
                for d in range(c, BLOCK):
                    x[c, d] = x[c, d] - f[c] * x[a, d] - f[d] * (x[a, c] - norm * f[c])
                    if d > c:
                        v[c, d] = v[c, d] - f[c] * v[a, d]
                y_row[c] = y_row[c] - f[c] * y_row[a]
                u_row[c] = u_row[c] - f[c] * u_row[a]
                y_col[c] = y_col[c] - tall(f[c], left) * y_col[a]
        if j + BLOCK < RANK:
            for a in range(BLOCK):
                y = y - y_col[a] * tall(inverse[a] * y_row[a], left)
                u = u - y_col[a] * tall(inverse[a] * u_row[a], left)
            if (j + BLOCK) % 8 == 0:
                y = y[j + BLOCK - base :, :]
                u = u[j + BLOCK - base :, :]
                base = j + BLOCK


def exchange_kernel(
    gate_hbm, up_hbm, out_grad_hbm, q_hbm,
    grad_ref, p_ref, q_all, p_turned_ref,
    g_buf, gate_buf, up_buf, h_buf, ht_buf, q_buf, qs_buf, proj_own, proj_out, proj_in, proj, coeff,
    p_part, p_in, p_all, q_part, q_in,
    local_sem, own_s, own_r, far_s, far_r, sib_s, sib_r, proj_s, proj_r, sum_s, sum_r, near_sem,
):
    dp = lax.axis_index("dp")
    tensor = lax.axis_index("tensor")
    z = tensor // 2
    core = lax.rem(tensor, 2)
    z_up, z_far, z_dn = lax.rem(z + 1, 4), lax.rem(z + 2, 4), lax.rem(z + 3, 4)
    t_up, t_far, t_dn = z_up * 2 + core, z_far * 2 + core, z_dn * 2 + core
    t_sib = z * 2 + 1 - core
    y = dp // 4
    x = lax.rem(dp, 4)
    offsets = sorted(
        ((a, b) for a in range(4) for b in range(4) if a or b),
        key=lambda o: -(min(o[0], 4 - o[0]) + min(o[1], 4 - o[1])),
    )
    peers = [lax.rem(y + a, 4) * 4 + lax.rem(x + b, 4) for a, b in offsets]

    def half_of(t, h):
        return pl.ds(pl.multiple_of(t * ROWS + h * HALF, HALF), HALF)

    def local_g(h):
        return pltpu.make_async_copy(
            out_grad_hbm.at[pl.ds(h * HALF, HALF), :], g_buf.at[half_of(tensor, h), :],
            local_sem.at[h])

    def local_in(k):
        src, dst = ((gate_hbm, gate_buf), (up_hbm, up_buf), (q_hbm, q_buf))[k]
        return pltpu.make_async_copy(src, dst, local_sem.at[2 + k])

    near = [
        y * 4 + lax.rem(x + 1, 4), y * 4 + lax.rem(x + 3, 4),
        lax.rem(y + 1, 4) * 4 + x, lax.rem(y + 3, 4) * 4 + x,
    ]
    barrier = pltpu.get_barrier_semaphore()
    for t in (t_up, t_dn, t_sib):
        pl.semaphore_signal(barrier, inc=1, device_id={"tensor": t}, device_id_type=MESH)
    for peer in near:
        pl.semaphore_signal(barrier, inc=1, device_id={"dp": peer}, device_id_type=MESH)
    for h in range(2):
        local_g(h).start()
    for k in range(3):
        local_in(k).start()
    pl.semaphore_wait(barrier, 3 + len(near))

    def tell(n):
        for peer in near:
            pl.semaphore_signal(
                near_sem.at[n], inc=1, device_id={"dp": peer}, device_id_type=MESH)

    def hear(n):
        pl.semaphore_wait(near_sem.at[n], len(near))

    def piece(t, h, to, send, recv):
        ref = g_buf.at[half_of(t, h), :]
        return pltpu.make_async_remote_copy(
            src_ref=ref, dst_ref=ref, send_sem=send, recv_sem=recv,
            device_id={"tensor": to}, device_id_type=MESH)

    def own(way, k):
        h = k if way == 0 else 1 - k
        return piece(tensor, h, (t_up, t_dn)[way], own_s.at[way, k], own_r.at[way, k])

    def onward(way):
        return piece((t_dn, t_up)[way], way, (t_up, t_dn)[way], far_s.at[way], far_r.at[way])

    def across(n, t, h):
        return piece(t, h, t_sib, sib_s.at[n], sib_r.at[n])

    for h in range(2):
        local_g(h).wait()
    for k in range(2):
        for way in range(2):
            own(way, k).start()
    for h in range(2):
        across(h, tensor, h).start()
    tell(0)

    local_in(0).wait()
    local_in(1).wait()

    def make_hidden(i, carry):
        rows = pl.ds(pl.multiple_of(i * 64, 64), 64)
        v = gate_buf[rows, :].astype(F32)
        w = up_buf[rows, :].astype(F32)
        h_buf[rows, :] = ((0.5 * v) * (1.0 + jnp.tanh(0.5 * v)) * w).astype(BF16)
        return carry

    lax.fori_loop(0, TOK // 64, make_hidden, 0)

    def turn_hidden(i, carry):
        cols = pl.ds(pl.multiple_of(i * TILE, TILE), TILE)
        ht_buf[cols, :] = h_buf[:, cols].T
        return carry

    lax.fori_loop(0, FF // TILE, turn_hidden, 0)
    def q_across():
        return pltpu.make_async_remote_copy(
            src_ref=qs_buf.at[pl.ds(0, 2 * RANK)], dst_ref=qs_buf.at[pl.ds(2 * RANK, 2 * RANK)],
            send_sem=proj_s.at[4], recv_sem=proj_r.at[4],
            device_id={"tensor": t_sib}, device_id_type=MESH)

    def proj_across(n):
        return pltpu.make_async_remote_copy(
            src_ref=proj_out.at[n], dst_ref=proj_in.at[n],
            send_sem=proj_s.at[n], recv_sem=proj_r.at[n],
            device_id={"tensor": t_sib}, device_id_type=MESH)

    def project(n, t):
        block = g_buf[pl.ds(pl.multiple_of(t * ROWS, ROWS), ROWS), :]
        both = dot(qs_buf[...], jnp.concatenate([block, block], axis=0), (1, 1))
        proj_own[n] = join2(both[: 2 * RANK])
        proj_out[n] = join2(both[2 * RANK :])
        proj_across(n).start()

    def crossed(n):
        across(n, tensor, 0).wait_recv()

    local_in(2).wait()
    qs_buf[: 2 * RANK, :] = split2(q_buf[...])
    q_across().start()
    hear(0)
    tell(1)
    q_across().wait_recv()
    project(0, tensor)
    for k in range(2):
        for way in range(2):
            own(way, k).wait_recv()
            if k == 0:
                onward(way).start()
            across(2 + 2 * k + way, (t_dn, t_up)[way], k if way == 0 else 1 - k).start()
        if k == 0:
            hear(1)
            tell(2)
    project(1, t_dn)
    project(2, t_up)
    hear(2)
    for way in range(2):
        onward(way).wait_recv()
        across(6 + way, t_far, way).start()
    project(3, t_far)

    def grad_tiles(first, last):
        def body(m, carry):
            rows = pl.ds(pl.multiple_of(m * GRAD_TILE, GRAD_TILE), GRAD_TILE)
            for c in range(0, D, WIDTH):
                cols = pl.ds(c, WIDTH)
                grad_ref[rows, cols] = dot(ht_buf[rows, :], g_buf[:, cols], (1, 0))
            return carry

        lax.fori_loop(first, last, body, 0)

    def scatter(part, landing, peer, n):
        return pltpu.make_async_remote_copy(
            src_ref=part.at[peer], dst_ref=landing.at[dp], send_sem=sum_s.at[n],
            recv_sem=sum_r.at[n], device_id={"dp": peer}, device_id_type=MESH)

    def gather(total, peer, n):
        return pltpu.make_async_remote_copy(
            src_ref=total.at[dp], dst_ref=total.at[dp], send_sem=sum_s.at[n],
            recv_sem=sum_r.at[n], device_id={"dp": peer}, device_id_type=MESH)

    def wait_all(ref, sem):
        ref = ref.at[pl.ds(0, DP - 1)]
        pltpu.make_async_copy(ref, ref, sem).wait()

    low_lanes = lax.broadcasted_iota(jnp.int32, (RANK, CHIP), 1) < ROWS
    mine = jnp.logical_xor(low_lanes, core == 1)
    for n, chip in enumerate((z, z_dn, z_up, z_far)):
        proj_across(n).wait_recv()
        cols = pl.ds(pl.multiple_of(chip * CHIP, CHIP), CHIP)
        turned = jnp.where(mine, proj_own[n], proj_in[n])
        proj[:, cols] = split2(turned)
    projected = proj[...]

    def p_slice(s):
        s = jnp.minimum(s, PSLICES - 1)
        cols = pl.ds(pl.multiple_of(s * PSLICE, PSLICE), PSLICE)
        return join2(dot(projected, h_buf[:, cols], (1, 0)))

    for peer in peers:
        p_part[peer] = p_slice(peer)
        scatter(p_part, p_in, peer, 0).start()
    p_in[dp] = p_slice(dp)
    for n in range(8):
        crossed(n)
    grad_tiles(0, FF // GRAD_TILE // 2)
    wait_all(p_in, sum_r.at[0])
    value = p_in[0]
    for s in range(1, DP):
        value = value + p_in[s]
    p_all[dp] = value
    for peer in peers:
        gather(p_all, peer, 1).start()
    grad_tiles(FF // GRAD_TILE // 2, FF // GRAD_TILE)
    wait_all(p_all, sum_r.at[1])

    power = jnp.concatenate([p_all[s] for s in range(PSLICES)], axis=1)
    gram = lax.dot_general(
        power, power, (((1,), (1,)), ((), ())), precision=HIGH, preferred_element_type=F32)
    mapped_power = join2(dot(split2(power), ht_buf[...], (1, 0)))
    gram_schmidt(gram, coeff)
    mapped = split2(
        jnp.dot(coeff[...], mapped_power, precision=HIGH, preferred_element_type=F32))

    def q_slice(s):
        cols = pl.ds(pl.multiple_of(s * QSLICE, QSLICE), QSLICE)
        return join2(dot(mapped, g_buf[:, cols], (1, 0))).astype(BF16)

    for peer in peers:
        q_part[peer] = q_slice(peer)
        scatter(q_part, q_in, peer, 2).start()
    q_in[dp] = q_slice(dp)
    basis = jnp.dot(coeff[...], power, precision=HIGH, preferred_element_type=F32)
    p_ref[...] = basis
    p_turned_ref[...] = split2(basis).T
    wait_all(q_in, sum_r.at[2])
    value = q_in[0].astype(F32)
    for s in range(1, DP):
        value = value + q_in[s].astype(F32)
    q_all[dp] = (value * (1.0 / DP)).astype(BF16)
    for peer in peers:
        gather(q_all, peer, 3).start()

    for way in range(2):
        for k in range(2):
            own(way, k).wait_send()
        onward(way).wait_send()
    for n in range(8):
        across(n, tensor, 0).wait_send()
    for n in range(4):
        proj_across(n).wait_send()
    q_across().wait_send()
    wait_all(p_part, sum_s.at[0])
    wait_all(p_all, sum_s.at[1])
    wait_all(q_part, sum_s.at[2])
    wait_all(q_all, sum_s.at[3])
    wait_all(q_all, sum_r.at[3])


def error_kernel(
    grad_ref, p_ref, q_ref, p_turned_ref, p_out, q_out, error_out,
    q2, q_wide, error_buf, sem, factor_sem,
):
    factors = (
        pltpu.make_async_copy(p_ref, p_out, factor_sem.at[0]),
        pltpu.make_async_copy(q_wide, q_out, factor_sem.at[1]),
    )
    for s in range(DP):
        q2[:, s * QSLICE : (s + 1) * QSLICE] = jnp.concatenate([q_ref[s], q_ref[s]], axis=0)
    copies = []
    for m in range(FF // ERROR_TILE):
        rows = pl.ds(m * ERROR_TILE, ERROR_TILE)
        for c in range(0, D, ERROR_WIDTH):
            cols = pl.ds(c, ERROR_WIDTH)
            low_rank = dot(p_turned_ref[rows, :], q2[:, cols], (1, 0))
            error_buf[rows, cols] = (grad_ref[rows, cols] - low_rank).astype(BF16)
        copies.append(
            pltpu.make_async_copy(error_buf.at[rows], error_out.at[rows], sem.at[m]))
        copies[-1].start()
        if m == 0:
            for s in range(DP):
                q_wide[:, s * QSLICE : (s + 1) * QSLICE] = q_ref[s].astype(F32)
            for copy in factors:
                copy.start()
    for copy in copies:
        copy.wait()
    for copy in factors:
        copy.wait()


def on_device(gate_pre, up_pre, out_grad, q_start):
    hbm_in = [
        pltpu.with_memory_space_constraint(v, pltpu.HBM)
        for v in (gate_pre, up_pre, out_grad, q_start[0].T)
    ]
    any_space = pl.BlockSpec(memory_space=pl.ANY)
    vmem_space = pl.BlockSpec(memory_space=pltpu.VMEM)
    dma = pltpu.SemaphoreType.DMA
    grad, p_factor, q_sums, p_turned = pl.pallas_call(
        exchange_kernel,
        out_shape=(
            pltpu.VMEM((FF, D), F32),
            pltpu.VMEM((RANK, FF), F32),
            pltpu.VMEM((DP, RANK, QSLICE), BF16),
            pltpu.VMEM((FF, 2 * RANK), BF16),
        ),
        in_specs=[any_space] * 4,
        out_specs=(vmem_space,) * 4,
        scratch_shapes=[
            pltpu.VMEM((TOK, D), BF16),
            pltpu.VMEM((TOK, FF), BF16),
            pltpu.VMEM((TOK, FF), BF16),
            pltpu.VMEM((TOK, FF), BF16),
            pltpu.VMEM((FF, TOK), BF16),
            pltpu.VMEM((RANK, D), F32),
            pltpu.VMEM((4 * RANK, D), BF16),
            pltpu.VMEM((4, RANK, CHIP), F32),
            pltpu.VMEM((4, RANK, CHIP), F32),
            pltpu.VMEM((4, RANK, CHIP), F32),
            pltpu.VMEM((2 * RANK, TOK), BF16),
            pltpu.VMEM((RANK, RANK), F32),
            pltpu.VMEM((DP, RANK, PSLICE), F32),
            pltpu.VMEM((DP, RANK, PSLICE), F32),
            pltpu.VMEM((DP, RANK, PSLICE), F32),
            pltpu.VMEM((DP, RANK, QSLICE), BF16),
            pltpu.VMEM((DP, RANK, QSLICE), BF16),
            dma((5,)),
            dma((2, 2)), dma((2, 2)), dma((2,)), dma((2,)),
            dma((8,)), dma((8,)), dma((5,)), dma((5,)), dma((4,)), dma((4,)),
            pltpu.SemaphoreType.REGULAR((3,)),
        ],
        compiler_params=pltpu.CompilerParams(
            collective_id=0, has_side_effects=True, vmem_limit_bytes=VMEM_BYTES),
        name="exchange",
    )(*hbm_in)
    p_out, q_out, new_error = pl.pallas_call(
        error_kernel,
        out_shape=(
            jax.ShapeDtypeStruct((RANK, FF), F32),
            jax.ShapeDtypeStruct((RANK, D), F32),
            jax.ShapeDtypeStruct((FF, D), BF16),
        ),
        in_specs=[vmem_space] * 4,
        out_specs=(any_space,) * 3,
        scratch_shapes=[
            pltpu.VMEM((2 * RANK, D), BF16),
            pltpu.VMEM((RANK, D), F32),
            pltpu.VMEM((FF, D), BF16),
            dma((FF // ERROR_TILE,)),
            dma((2,)),
        ],
        compiler_params=pltpu.CompilerParams(vmem_limit_bytes=VMEM_BYTES),
        name="error",
    )(grad, p_factor, q_sums, p_turned)
    return (p_out.T, q_out.T[None], new_error[None])


def solution(mesh):
    placed = (
        P("dp", "tensor"),
        P("dp", "tensor"),
        P(("dp", "tensor"), None),
        P("tensor", None, None),
    )
    return jax.shard_map(
        on_device,
        mesh=mesh,
        in_specs=placed,
        out_specs=(P("tensor", None), P("tensor", None, None), P("dp", "tensor", None)),
        check_vma=False,
    )
```

```python
import functools

import jax
import jax.numpy as jnp
from jax import lax
from jax.experimental import pallas as pl
from jax.experimental.pallas import tpu as pltpu
from jax.sharding import PartitionSpec as P

EPSILON = 1e-06
HIGH = lax.Precision.HIGHEST
BF16 = jnp.bfloat16
F32 = jnp.float32
MESH = pl.DeviceIdType.MESH

TOK = 512
ROWS = 64
D = 4096
FF = 1792
RANK = 32
HALF = ROWS // 2
CHIP = 2 * ROWS
Q_HALF = 16
DP = 16
PSLICE = 128
PSLICES = FF // PSLICE
QSLICE = D // DP
TILE = 256
WIDTH = 512
GRAD_TILE = 448
BLOCK = 4
ERROR_TILE = 128
ERROR_WIDTH = 256
VMEM_BYTES = 24 * 2**20


def dot(a, b, contract):
    return lax.dot_general(a, b, ((contract[:1], contract[1:]), ((), ())), preferred_element_type=F32)


def split2(x):
    high = x.astype(BF16)
    low = (x - high.astype(F32)).astype(BF16)
    return jnp.concatenate([high, low], axis=0)


def join2(x):
    return x[:RANK] + x[RANK:]


def gram_schmidt(gram, coeff_ref):
    rows = lax.broadcasted_iota(jnp.int32, (RANK, RANK), 0)
    cols = lax.broadcasted_iota(jnp.int32, (RANK, RANK), 1)
    y = gram
    u = jnp.where(rows == cols, 1.0, 0.0).astype(F32)
    base = 0

    def spread_row(m, r):
        return jnp.broadcast_to(m[r : r + 1, :], (8, RANK))

    def tall(m, n):
        return jnp.concatenate([m] * (n // 8), axis=0) if n > 8 else m

    for j in range(0, RANK, BLOCK):
        at = j - base
        left = RANK - base
        y_row = [spread_row(y, at + a) for a in range(BLOCK)]
        u_row = [spread_row(u, at + a) for a in range(BLOCK)]
        y_col = [jnp.broadcast_to(y[:, j + a : j + a + 1], (left, RANK)) for a in range(BLOCK)]
        pairs = [(a, c) for a in range(BLOCK) for c in range(a, BLOCK)]
        x = {
            (a, c): jnp.broadcast_to(
                jnp.sum(u_row[a] * y_row[c], axis=1, keepdims=True), (8, RANK))
            for a, c in pairs
        }
        v = {(a, c): spread_row(y_col[a], at + c) for a, c in pairs if c > a}
        inverse = []
        for a in range(BLOCK):
            norm = x[a, a]
            scale = lax.rsqrt(jnp.maximum(norm, 0.0) + EPSILON)
            inverse.append(scale * scale)
            coeff_ref[j + a : j + a + 1, :] = (u_row[a] * scale)[:1]
            f = {c: v[a, c] * inverse[a] for c in range(a + 1, BLOCK)}
            for c in range(a + 1, BLOCK):
                for d in range(c, BLOCK):
                    x[c, d] = x[c, d] - f[c] * x[a, d] - f[d] * (x[a, c] - norm * f[c])
                    if d > c:
                        v[c, d] = v[c, d] - f[c] * v[a, d]
                y_row[c] = y_row[c] - f[c] * y_row[a]
                u_row[c] = u_row[c] - f[c] * u_row[a]
                y_col[c] = y_col[c] - tall(f[c], left) * y_col[a]
        if j + BLOCK < RANK:
            for a in range(BLOCK):
                y = y - y_col[a] * tall(inverse[a] * y_row[a], left)
                u = u - y_col[a] * tall(inverse[a] * u_row[a], left)
            if (j + BLOCK) % 8 == 0:
                y = y[j + BLOCK - base :, :]
                u = u[j + BLOCK - base :, :]
                base = j + BLOCK


def exchange_kernel(
    gate_hbm, up_hbm, out_grad_hbm, q_hbm,
    grad_ref, p_ref, q_all, p_turned_ref,
    g_buf, gate_buf, up_buf, h_buf, ht_buf, q_buf, q_ring, proj_out, proj_in, proj, coeff,
    p_part, p_in, p_all, q_part, q_in,
    local_sem, q_own_s, q_own_r, q_far_s, q_far_r, own_s, own_r, far_s, far_r, sib_s, sib_r,
    proj_s, proj_r, sum_s, sum_r, near_sem,
):
    dp = lax.axis_index("dp")
    tensor = lax.axis_index("tensor")
    z = tensor // 2
    core = lax.rem(tensor, 2)
    z_up, z_far, z_dn = lax.rem(z + 1, 4), lax.rem(z + 2, 4), lax.rem(z + 3, 4)
    t_up, t_far, t_dn = z_up * 2 + core, z_far * 2 + core, z_dn * 2 + core
    t_sib = z * 2 + 1 - core
    y = dp // 4
    x = lax.rem(dp, 4)
    offsets = sorted(
        ((a, b) for a in range(4) for b in range(4) if a or b),
        key=lambda o: -(min(o[0], 4 - o[0]) + min(o[1], 4 - o[1])),
    )
    peers = [lax.rem(y + a, 4) * 4 + lax.rem(x + b, 4) for a, b in offsets]

    def half_of(t, h):
        return pl.ds(pl.multiple_of(t * ROWS + h * HALF, HALF), HALF)

    def local_g(h):
        return pltpu.make_async_copy(
            out_grad_hbm.at[pl.ds(h * HALF, HALF), :], g_buf.at[half_of(tensor, h), :],
            local_sem.at[h])

    def local_in(k):
        src, dst = ((gate_hbm, gate_buf), (up_hbm, up_buf), (q_hbm, q_buf))[k]
        return pltpu.make_async_copy(src, dst, local_sem.at[2 + k])

    near = [
        y * 4 + lax.rem(x + 1, 4), y * 4 + lax.rem(x + 3, 4),
        lax.rem(y + 1, 4) * 4 + x, lax.rem(y + 3, 4) * 4 + x,
    ]
    barrier = pltpu.get_barrier_semaphore()
    for t in (t_up, t_dn, t_sib):
        pl.semaphore_signal(barrier, inc=1, device_id={"tensor": t}, device_id_type=MESH)
    for peer in near:
        pl.semaphore_signal(barrier, inc=1, device_id={"dp": peer}, device_id_type=MESH)
    local_in(2).start()
    for h in range(2):
        local_g(h).start()
    for k in range(2):
        local_in(k).start()
    local_in(2).wait()
    q_ring[z] = q_buf[...].astype(BF16)
    pl.semaphore_wait(barrier, 3 + len(near))

    def tell(n):
        for peer in near:
            pl.semaphore_signal(
                near_sem.at[n], inc=1, device_id={"dp": peer}, device_id_type=MESH)

    def hear(n):
        pl.semaphore_wait(near_sem.at[n], len(near))

    def piece(t, h, to, send, recv):
        ref = g_buf.at[half_of(t, h), :]
        return pltpu.make_async_remote_copy(
            src_ref=ref, dst_ref=ref, send_sem=send, recv_sem=recv,
            device_id={"tensor": to}, device_id_type=MESH)

    def own(way, k):
        h = (way, way, 1 - way)[k]
        start, size = ((0, HALF // 2), (HALF // 2, HALF // 2), (0, HALF))[k]
        ref = g_buf.at[pl.ds(pl.multiple_of(tensor * ROWS + h * HALF + start, HALF // 2), size), :]
        return pltpu.make_async_remote_copy(
            src_ref=ref, dst_ref=ref, send_sem=own_s.at[way, k], recv_sem=own_r.at[way, k],
            device_id={"tensor": (t_up, t_dn)[way]}, device_id_type=MESH)

    def onward(way):
        return piece((t_dn, t_up)[way], way, (t_up, t_dn)[way], far_s.at[way], far_r.at[way])

    def across(n, t, h):
        return piece(t, h, t_sib, sib_s.at[n], sib_r.at[n])

    def q_piece(chip, h, to, send, recv):
        ref = q_ring.at[chip, pl.ds(h * Q_HALF, Q_HALF), :]
        return pltpu.make_async_remote_copy(
            src_ref=ref, dst_ref=ref, send_sem=send, recv_sem=recv,
            device_id={"tensor": to}, device_id_type=MESH)

    def q_own(way, k):
        h = k if way == 0 else 1 - k
        return q_piece(z, h, (t_up, t_dn)[way], q_own_s.at[way, k], q_own_r.at[way, k])

    def q_onward(way):
        return q_piece(
            (z_dn, z_up)[way], way, (t_up, t_dn)[way], q_far_s.at[way], q_far_r.at[way])

    for k in range(2):
        for way in range(2):
            q_own(way, k).start()
    tell(0)
    for h in range(2):
        local_g(h).wait()
        across(h, tensor, h).start()
    for way in range(2):
        q_own(way, 0).wait_recv()
        q_onward(way).start()
    for way in range(2):
        own(way, 0).start()

    local_in(0).wait()
    local_in(1).wait()

    def make_hidden(i, carry):
        rows = pl.ds(pl.multiple_of(i * 64, 64), 64)
        v = gate_buf[rows, :].astype(F32)
        w = up_buf[rows, :].astype(F32)
        h_buf[rows, :] = ((0.5 * v) * (1.0 + jnp.tanh(0.5 * v)) * w).astype(BF16)
        return carry

    lax.fori_loop(0, TOK // 64, make_hidden, 0)

    def turn_hidden(i, carry):
        cols = pl.ds(pl.multiple_of(i * TILE, TILE), TILE)
        ht_buf[cols, :] = h_buf[:, cols].T
        return carry

    lax.fori_loop(0, FF // TILE, turn_hidden, 0)
    chip_rows = pl.ds(pl.multiple_of(z * CHIP, CHIP), CHIP)

    def project(chip):
        return dot(q_ring[chip], g_buf[chip_rows, :], (1, 1))

    def proj_send(n, to):
        return pltpu.make_async_remote_copy(
            src_ref=proj_out.at[n], dst_ref=proj_in.at[z], send_sem=proj_s.at[n],
            recv_sem=proj_r.at[n], device_id={"tensor": to}, device_id_type=MESH)

    def crossed(n):
        across(n, tensor, 0).wait_recv()

    def pass_on(k):
        for way in range(2):
            if k == 0:
                own(way, 0).wait_recv()
                own(way, 1).wait_recv()
                onward(way).start()
            else:
                own(way, 2).wait_recv()
            across(2 + 2 * k + way, (t_dn, t_up)[way], k if way == 0 else 1 - k).start()

    hear(0)
    tell(1)
    crossed(0)
    crossed(1)
    proj_in[z] = project(z)
    for way in range(2):
        q_own(way, 1).wait_recv()
    for n, (chip, to) in enumerate(((z_up, t_up), (z_dn, t_dn))):
        proj_out[n] = project(chip)
        proj_send(n, to).start()
    for way in range(2):
        q_onward(way).wait_recv()
    proj_out[2] = project(z_far)
    proj_send(2, t_far).start()
    for k in (1, 2):
        for way in range(2):
            own(way, k).start()
    hear(1)
    tell(2)

    def grad_tiles(first, last):
        def body(m, carry):
            rows = pl.ds(pl.multiple_of(m * GRAD_TILE, GRAD_TILE), GRAD_TILE)
            for c in range(0, D, WIDTH):
                cols = pl.ds(c, WIDTH)
                grad_ref[rows, cols] = dot(ht_buf[rows, :], g_buf[:, cols], (1, 0))
            return carry

        lax.fori_loop(first, last, body, 0)

    def scatter(part, landing, peer, n):
        return pltpu.make_async_remote_copy(
            src_ref=part.at[peer], dst_ref=landing.at[dp], send_sem=sum_s.at[n],
            recv_sem=sum_r.at[n], device_id={"dp": peer}, device_id_type=MESH)

    def gather(total, peer, n):
        return pltpu.make_async_remote_copy(
            src_ref=total.at[dp], dst_ref=total.at[dp], send_sem=sum_s.at[n],
            recv_sem=sum_r.at[n], device_id={"dp": peer}, device_id_type=MESH)

    def wait_all(ref, sem):
        ref = ref.at[pl.ds(0, DP - 1)]
        pltpu.make_async_copy(ref, ref, sem).wait()

    for n, (chip, to) in enumerate(((z_dn, t_up), (z_up, t_dn), (z_far, t_far), (z, None))):
        if to is not None:
            proj_send(n, to).wait_recv()
        cols = pl.ds(pl.multiple_of(chip * CHIP, CHIP), CHIP)
        proj[:, cols] = split2(proj_in[chip])
    projected = proj[...]
    hear(2)

    def p_slice(s):
        s = jnp.minimum(s, PSLICES - 1)
        cols = pl.ds(pl.multiple_of(s * PSLICE, PSLICE), PSLICE)
        return join2(dot(projected, h_buf[:, cols], (1, 0)))

    for peer in peers:
        p_part[peer] = p_slice(peer)
        scatter(p_part, p_in, peer, 0).start()
    p_in[dp] = p_slice(dp)
    pass_on(0)
    wait_all(p_in, sum_r.at[0])
    value = p_in[0]
    for s in range(1, DP):
        value = value + p_in[s]
    p_all[dp] = value
    for peer in peers:
        gather(p_all, peer, 1).start()
    pass_on(1)
    wait_all(p_all, sum_r.at[1])

    power = jnp.concatenate([p_all[s] for s in range(PSLICES)], axis=1)
    gram = lax.dot_general(
        power, power, (((1,), (1,)), ((), ())), precision=HIGH, preferred_element_type=F32)
    mapped_power = join2(dot(split2(power), ht_buf[...], (1, 0)))
    gram_schmidt(gram, coeff)
    mapped = split2(
        jnp.dot(coeff[...], mapped_power, precision=HIGH, preferred_element_type=F32))

    for way in range(2):
        onward(way).wait_recv()
        across(6 + way, t_far, way).start()
    for n in range(2, 8):
        crossed(n)

    def q_slice(s):
        cols = pl.ds(pl.multiple_of(s * QSLICE, QSLICE), QSLICE)
        return join2(dot(mapped, g_buf[:, cols], (1, 0))).astype(BF16)

    for peer in peers:
        q_part[peer] = q_slice(peer)
        scatter(q_part, q_in, peer, 2).start()
    q_in[dp] = q_slice(dp)
    grad_tiles(0, FF // GRAD_TILE // 2)
    wait_all(q_in, sum_r.at[2])
    value = q_in[0].astype(F32)
    for s in range(1, DP):
        value = value + q_in[s].astype(F32)
    q_all[dp] = (value * (1.0 / DP)).astype(BF16)
    for peer in peers:
        gather(q_all, peer, 3).start()
    basis = jnp.dot(coeff[...], power, precision=HIGH, preferred_element_type=F32)
    p_ref[...] = basis
    p_turned_ref[...] = split2(basis).T
    grad_tiles(FF // GRAD_TILE // 2, FF // GRAD_TILE)

    for way in range(2):
        for k in range(3):
            own(way, k).wait_send()
        for k in range(2):
            q_own(way, k).wait_send()
        onward(way).wait_send()
        q_onward(way).wait_send()
    for n in range(8):
        across(n, tensor, 0).wait_send()
    for n in range(3):
        proj_send(n, t_up).wait_send()
    wait_all(p_part, sum_s.at[0])
    wait_all(p_all, sum_s.at[1])
    wait_all(q_part, sum_s.at[2])
    wait_all(q_all, sum_s.at[3])
    wait_all(q_all, sum_r.at[3])


def error_kernel(
    grad_ref, p_ref, q_ref, p_turned_ref, p_out, q_out, error_out,
    q2, q_wide, error_buf, sem, factor_sem,
):
    factors = (
        pltpu.make_async_copy(p_ref, p_out, factor_sem.at[0]),
        pltpu.make_async_copy(q_wide, q_out, factor_sem.at[1]),
    )
    for s in range(DP):
        q2[:, s * QSLICE : (s + 1) * QSLICE] = jnp.concatenate([q_ref[s], q_ref[s]], axis=0)
    copies = []
    for m in range(FF // ERROR_TILE):
        rows = pl.ds(m * ERROR_TILE, ERROR_TILE)
        for c in range(0, D, ERROR_WIDTH):
            cols = pl.ds(c, ERROR_WIDTH)
            low_rank = dot(p_turned_ref[rows, :], q2[:, cols], (1, 0))
            error_buf[rows, cols] = (grad_ref[rows, cols] - low_rank).astype(BF16)
        copies.append(
            pltpu.make_async_copy(error_buf.at[rows], error_out.at[rows], sem.at[m]))
        copies[-1].start()
        if m == 0:
            for s in range(DP):
                q_wide[:, s * QSLICE : (s + 1) * QSLICE] = q_ref[s].astype(F32)
            for copy in factors:
                copy.start()
    for copy in copies:
        copy.wait()
    for copy in factors:
        copy.wait()


def on_device(gate_pre, up_pre, out_grad, q_start):
    hbm_in = [
        pltpu.with_memory_space_constraint(v, pltpu.HBM)
        for v in (gate_pre, up_pre, out_grad, q_start[0].T)
    ]
    any_space = pl.BlockSpec(memory_space=pl.ANY)
    vmem_space = pl.BlockSpec(memory_space=pltpu.VMEM)
    dma = pltpu.SemaphoreType.DMA
    grad, p_factor, q_sums, p_turned = pl.pallas_call(
        exchange_kernel,
        out_shape=(
            pltpu.VMEM((FF, D), F32),
            pltpu.VMEM((RANK, FF), F32),
            pltpu.VMEM((DP, RANK, QSLICE), BF16),
            pltpu.VMEM((FF, 2 * RANK), BF16),
        ),
        in_specs=[any_space] * 4,
        out_specs=(vmem_space,) * 4,
        scratch_shapes=[
            pltpu.VMEM((TOK, D), BF16),
            pltpu.VMEM((TOK, FF), BF16),
            pltpu.VMEM((TOK, FF), BF16),
            pltpu.VMEM((TOK, FF), BF16),
            pltpu.VMEM((FF, TOK), BF16),
            pltpu.VMEM((RANK, D), F32),
            pltpu.VMEM((4, RANK, D), BF16),
            pltpu.VMEM((3, RANK, CHIP), F32),
            pltpu.VMEM((4, RANK, CHIP), F32),
            pltpu.VMEM((2 * RANK, TOK), BF16),
            pltpu.VMEM((RANK, RANK), F32),
            pltpu.VMEM((DP, RANK, PSLICE), F32),
            pltpu.VMEM((DP, RANK, PSLICE), F32),
            pltpu.VMEM((DP, RANK, PSLICE), F32),
            pltpu.VMEM((DP, RANK, QSLICE), BF16),
            pltpu.VMEM((DP, RANK, QSLICE), BF16),
            dma((5,)),
            dma((2, 2)), dma((2, 2)), dma((2,)), dma((2,)),
            dma((2, 3)), dma((2, 3)), dma((2,)), dma((2,)),
            dma((8,)), dma((8,)), dma((3,)), dma((3,)), dma((4,)), dma((4,)),
            pltpu.SemaphoreType.REGULAR((3,)),
        ],
        compiler_params=pltpu.CompilerParams(
            collective_id=0, has_side_effects=True, vmem_limit_bytes=VMEM_BYTES),
        name="exchange",
    )(*hbm_in)
    p_out, q_out, new_error = pl.pallas_call(
        error_kernel,
        out_shape=(
            jax.ShapeDtypeStruct((RANK, FF), F32),
            jax.ShapeDtypeStruct((RANK, D), F32),
            jax.ShapeDtypeStruct((FF, D), BF16),
        ),
        in_specs=[vmem_space] * 4,
        out_specs=(any_space,) * 3,
        scratch_shapes=[
            pltpu.VMEM((2 * RANK, D), BF16),
            pltpu.VMEM((RANK, D), F32),
            pltpu.VMEM((FF, D), BF16),
            dma((FF // ERROR_TILE,)),
            dma((2,)),
        ],
        compiler_params=pltpu.CompilerParams(vmem_limit_bytes=VMEM_BYTES),
        name="error",
    )(grad, p_factor, q_sums, p_turned)
    return (p_out.T, q_out.T[None], new_error[None])


def solution(mesh):
    placed = (
        P("dp", "tensor"),
        P("dp", "tensor"),
        P(("dp", "tensor"), None),
        P("tensor", None, None),
    )
    return jax.shard_map(
        on_device,
        mesh=mesh,
        in_specs=placed,
        out_specs=(P("tensor", None), P("tensor", None, None), P("dp", "tensor", None)),
        check_vma=False,
    )
```

```python
import functools

import jax
import jax.numpy as jnp
from jax import lax
from jax.experimental import pallas as pl
from jax.experimental.pallas import tpu as pltpu
from jax.sharding import PartitionSpec as P

EPSILON = 1e-06
HIGH = lax.Precision.HIGHEST
BF16 = jnp.bfloat16
F32 = jnp.float32
MESH = pl.DeviceIdType.MESH

TOK = 512
ROWS = 64
D = 4096
FF = 1792
RANK = 32
HALF = ROWS // 2
CHIP = 2 * ROWS
Q_HALF = 16
PART = HALF // 2
DP = 16
PSLICE = 128
PSLICES = FF // PSLICE
QSLICE = D // DP
LINE = 4 * QSLICE
RING = D - 2 * LINE
EARLY = 2
TILE = 256
WIDTH = 512
GRAD_TILE = 448
BLOCK = 4
ERROR_TILE = 128
ERROR_WIDTH = 256
VMEM_BYTES = 24 * 2**20


def dot(a, b, contract):
    return lax.dot_general(a, b, ((contract[:1], contract[1:]), ((), ())), preferred_element_type=F32)


def split2(x):
    high = x.astype(BF16)
    low = (x - high.astype(F32)).astype(BF16)
    return jnp.concatenate([high, low], axis=0)


def join2(x):
    return x[:RANK] + x[RANK:]


def gram_schmidt(gram, coeff_ref):
    rows = lax.broadcasted_iota(jnp.int32, (RANK, RANK), 0)
    cols = lax.broadcasted_iota(jnp.int32, (RANK, RANK), 1)
    y = gram
    u = jnp.where(rows == cols, 1.0, 0.0).astype(F32)
    base = 0

    def spread_row(m, r):
        return jnp.broadcast_to(m[r : r + 1, :], (8, RANK))

    def tall(m, n):
        return jnp.concatenate([m] * (n // 8), axis=0) if n > 8 else m

    for j in range(0, RANK, BLOCK):
        at = j - base
        left = RANK - base
        y_row = [spread_row(y, at + a) for a in range(BLOCK)]
        u_row = [spread_row(u, at + a) for a in range(BLOCK)]
        y_col = [jnp.broadcast_to(y[:, j + a : j + a + 1], (left, RANK)) for a in range(BLOCK)]
        pairs = [(a, c) for a in range(BLOCK) for c in range(a, BLOCK)]
        x = {
            (a, c): jnp.broadcast_to(
                jnp.sum(u_row[a] * y_row[c], axis=1, keepdims=True), (8, RANK))
            for a, c in pairs
        }
        v = {(a, c): spread_row(y_col[a], at + c) for a, c in pairs if c > a}
        inverse = []
        for a in range(BLOCK):
            norm = x[a, a]
            scale = lax.rsqrt(jnp.maximum(norm, 0.0) + EPSILON)
            inverse.append(scale * scale)
            coeff_ref[j + a : j + a + 1, :] = (u_row[a] * scale)[:1]
            f = {c: v[a, c] * inverse[a] for c in range(a + 1, BLOCK)}
            for c in range(a + 1, BLOCK):
                for d in range(c, BLOCK):
                    x[c, d] = x[c, d] - f[c] * x[a, d] - f[d] * (x[a, c] - norm * f[c])
                    if d > c:
                        v[c, d] = v[c, d] - f[c] * v[a, d]
                y_row[c] = y_row[c] - f[c] * y_row[a]
                u_row[c] = u_row[c] - f[c] * u_row[a]
                y_col[c] = y_col[c] - tall(f[c], left) * y_col[a]
        if j + BLOCK < RANK:
            for a in range(BLOCK):
                y = y - y_col[a] * tall(inverse[a] * y_row[a], left)
                u = u - y_col[a] * tall(inverse[a] * u_row[a], left)
            if (j + BLOCK) % 8 == 0:
                y = y[j + BLOCK - base :, :]
                u = u[j + BLOCK - base :, :]
                base = j + BLOCK


def exchange_kernel(
    gate_hbm, up_hbm, out_grad_hbm, q_hbm,
    grad_ref, p_ref, q_all, p_turned_ref,
    g_buf, gate_buf, up_buf, h_buf, ht_buf, q_buf, q_ring, q_cross, proj_out, proj_in, proj, coeff,
    p_part, p_in, p_all, q_part, q_in,
    local_sem, pull_s, pull_r, cross_s, cross_r, q_own_s, q_own_r, q_far_s, q_far_r, own_s, own_r, far_s, far_r,
    sib_s, sib_r, far_sib_s, far_sib_r, proj_s, proj_r, sum_s, sum_r, near_sem,
):
    dp = lax.axis_index("dp")
    tensor = lax.axis_index("tensor")
    z = tensor // 2
    core = lax.rem(tensor, 2)
    z_up, z_far, z_dn = lax.rem(z + 1, 4), lax.rem(z + 2, 4), lax.rem(z + 3, 4)
    t_up, t_far, t_dn = z_up * 2 + core, z_far * 2 + core, z_dn * 2 + core
    t_sib = z * 2 + 1 - core
    y = dp // 4
    x = lax.rem(dp, 4)
    hops = {
        (a, b): min(a, 4 - a) + min(b, 4 - b) for a in range(4) for b in range(4) if a or b
    }
    peer_at = {
        o: lax.rem(y + o[0], 4) * 4 + lax.rem(x + o[1], 4)
        for o in sorted(hops, key=lambda o: -hops[o])
    }
    peers = list(peer_at.values())
    near = [peer_at[o] for o in peer_at if hops[o] == 1]
    opposite = [peer_at[0, 2], peer_at[2, 0]]
    lines = ([peer_at[0, k] for k in (2, 1, 3)], [peer_at[k, 0] for k in (2, 1, 3)])

    def half_of(t, h):
        return pl.ds(pl.multiple_of(t * ROWS + h * HALF, HALF), HALF)

    def local_g(h):
        return pltpu.make_async_copy(
            out_grad_hbm.at[pl.ds(h * HALF, HALF), :], g_buf.at[half_of(tensor, h), :],
            local_sem.at[h])

    def local_in(k):
        src, dst = ((gate_hbm, gate_buf), (up_hbm, up_buf), (q_hbm, q_buf))[k]
        return pltpu.make_async_copy(src, dst, local_sem.at[2 + k])

    barrier = pltpu.get_barrier_semaphore()
    for t in (t_up, t_dn, t_far, t_sib):
        pl.semaphore_signal(barrier, inc=1, device_id={"tensor": t}, device_id_type=MESH)
    for peer in near:
        pl.semaphore_signal(barrier, inc=1, device_id={"dp": peer}, device_id_type=MESH)
    local_in(2).start()
    for h in range(2):
        local_g(h).start()
    for k in range(2):
        local_in(k).start()
    local_in(2).wait()
    q_ring[0] = q_buf[:, :RING].astype(BF16)
    for line in range(2):
        for k in range(4):
            col = RING + line * LINE + k * QSLICE
            q_cross[line, k, 0] = q_buf[:, col : col + QSLICE].astype(BF16)
    pl.semaphore_wait(barrier, 4 + len(near))

    def tell(n):
        for peer in (near, opposite)[n]:
            pl.semaphore_signal(
                near_sem.at[n], inc=1, device_id={"dp": peer}, device_id_type=MESH)

    def hear(n):
        pl.semaphore_wait(near_sem.at[n], (len(near), len(opposite))[n])

    def pull(n, line):
        to, place = ((t_up, 3), (t_dn, 1), (t_far, 2))[n]
        part = q_cross.at[line, (x, y)[line]]
        return pltpu.make_async_remote_copy(
            src_ref=part.at[0], dst_ref=part.at[place], send_sem=pull_s.at[n, line],
            recv_sem=pull_r.at[n, line], device_id={"tensor": to}, device_id_type=MESH)

    def spread(line, peer):
        ref = q_cross.at[line, (x, y)[line], pl.ds(1, 3)]
        return pltpu.make_async_remote_copy(
            src_ref=ref, dst_ref=ref, send_sem=cross_s.at[line], recv_sem=cross_r.at[line],
            device_id={"dp": peer}, device_id_type=MESH)

    def spread_wait(line, sem):
        ref = q_cross.at[line, pl.ds(0, 3), pl.ds(1, 3)]
        pltpu.make_async_copy(ref, ref, sem.at[line]).wait()

    def piece(t, h, to, send, recv):
        ref = g_buf.at[half_of(t, h), :]
        return pltpu.make_async_remote_copy(
            src_ref=ref, dst_ref=ref, send_sem=send, recv_sem=recv,
            device_id={"tensor": to}, device_id_type=MESH)

    pieces = ((0, PART, 0, D // 2), (0, PART, D // 2, D // 2), (PART, PART, 0, D), (0, HALF, 0, D))

    def own(way, k):
        h = 1 - way if k == 3 else way
        row, rows, col, cols = pieces[k]
        ref = g_buf.at[
            pl.ds(pl.multiple_of(tensor * ROWS + h * HALF + row, PART), rows), pl.ds(col, cols)]
        return pltpu.make_async_remote_copy(
            src_ref=ref, dst_ref=ref, send_sem=own_s.at[way, k], recv_sem=own_r.at[way, k],
            device_id={"tensor": (t_up, t_dn)[way]}, device_id_type=MESH)

    def part_of(t, h, part):
        return g_buf.at[pl.ds(pl.multiple_of(t * ROWS + h * HALF + part * PART, PART), PART), :]

    def onward(way, part):
        ref = part_of((t_dn, t_up)[way], way, part)
        return pltpu.make_async_remote_copy(
            src_ref=ref, dst_ref=ref, send_sem=far_s.at[way, part], recv_sem=far_r.at[way, part],
            device_id={"tensor": (t_up, t_dn)[way]}, device_id_type=MESH)

    def far_across(way, part):
        ref = part_of(t_far, way, part)
        return pltpu.make_async_remote_copy(
            src_ref=ref, dst_ref=ref, send_sem=far_sib_s.at[way, part],
            recv_sem=far_sib_r.at[way, part], device_id={"tensor": t_sib}, device_id_type=MESH)

    def across(n, t, h):
        return piece(t, h, t_sib, sib_s.at[n], sib_r.at[n])

    def q_piece(source, place, h, to, send, recv):
        rows = pl.ds(h * Q_HALF, Q_HALF)
        return pltpu.make_async_remote_copy(
            src_ref=q_ring.at[source, rows, :], dst_ref=q_ring.at[place, rows, :],
            send_sem=send, recv_sem=recv, device_id={"tensor": to}, device_id_type=MESH)

    def q_own(way, k):
        h = k if way == 0 else 1 - k
        return q_piece(
            0, (3, 1)[way], h, (t_up, t_dn)[way], q_own_s.at[way, k], q_own_r.at[way, k])

    def q_onward(way):
        return q_piece((3, 1)[way], 2, way, (t_up, t_dn)[way], q_far_s.at[way], q_far_r.at[way])

    for n in range(3):
        for line in range(2):
            pull(n, line).start()
    for k in range(2):
        for way in range(2):
            q_own(way, k).start()
    tell(0)
    for h in range(2):
        local_g(h).wait()
        across(h, tensor, h).start()
    hear(0)
    tell(1)
    for line in range(2):
        for n in range(3):
            pull(n, line).wait_recv()
        for peer in lines[line]:
            spread(line, peer).start()
    for way in range(2):
        q_own(way, 0).wait_recv()
        q_onward(way).start()
    for k in range(EARLY):
        for way in range(2):
            own(way, k).start()

    local_in(0).wait()
    local_in(1).wait()

    def make_hidden(i, carry):
        rows = pl.ds(pl.multiple_of(i * 64, 64), 64)
        v = gate_buf[rows, :].astype(F32)
        w = up_buf[rows, :].astype(F32)
        h_buf[rows, :] = ((0.5 * v) * (1.0 + jnp.tanh(0.5 * v)) * w).astype(BF16)
        return carry

    lax.fori_loop(0, TOK // 64, make_hidden, 0)

    def turn_hidden(i, carry):
        cols = pl.ds(pl.multiple_of(i * TILE, TILE), TILE)
        ht_buf[cols, :] = h_buf[:, cols].T
        return carry

    lax.fori_loop(0, FF // TILE, turn_hidden, 0)
    chip_rows = pl.ds(pl.multiple_of(z * CHIP, CHIP), CHIP)

    def proj_send(n, to):
        return pltpu.make_async_remote_copy(
            src_ref=proj_out.at[n], dst_ref=proj_in.at[z], send_sem=proj_s.at[n],
            recv_sem=proj_r.at[n], device_id={"tensor": to}, device_id_type=MESH)

    def crossed(n):
        across(n, tensor, 0).wait_recv()

    def pass_on(k):
        for way in range(2):
            if k == 0:
                own(way, 0).wait_recv()
                own(way, 1).wait_recv()
                onward(way, 0).start()
            else:
                own(way, 3).wait_recv()
                across(4 + way, (t_dn, t_up)[way], 1 - way).start()
        if k == 0:
            for way in range(2):
                own(way, 2).wait_recv()
                onward(way, 1).start()
                across(2 + way, (t_dn, t_up)[way], way).start()

    crossed(0)
    crossed(1)
    for way in range(2):
        q_own(way, 1).wait_recv()
        q_onward(way).wait_recv()
    results = dot(q_ring[...].reshape(4 * RANK, RING), g_buf[chip_rows, :RING], (1, 1))
    for line in range(2):
        spread_wait(line, cross_r)
        for k in range(4):
            col = RING + line * LINE + k * QSLICE
            results += dot(
                q_cross[line, k].reshape(4 * RANK, QSLICE), g_buf[chip_rows, col : col + QSLICE],
                (1, 1))
    proj_in[z] = results[:RANK]
    for n, (place, to) in enumerate(((1, t_up), (3, t_dn), (2, t_far))):
        proj_out[n] = results[place * RANK : (place + 1) * RANK]
    for n, to in ((2, t_far), (0, t_up), (1, t_dn)):
        proj_send(n, to).start()
    for k in range(EARLY, 4):
        for way in range(2):
            own(way, k).start()
    hear(1)

    def grad_tiles(first, last):
        def body(m, carry):
            rows = pl.ds(pl.multiple_of(m * GRAD_TILE, GRAD_TILE), GRAD_TILE)
            for c in range(0, D, WIDTH):
                cols = pl.ds(c, WIDTH)
                grad_ref[rows, cols] = dot(ht_buf[rows, :], g_buf[:, cols], (1, 0))
            return carry

        lax.fori_loop(first, last, body, 0)

    def scatter(part, landing, peer, n):
        return pltpu.make_async_remote_copy(
            src_ref=part.at[peer], dst_ref=landing.at[dp], send_sem=sum_s.at[n],
            recv_sem=sum_r.at[n], device_id={"dp": peer}, device_id_type=MESH)

    def gather(total, peer, n):
        return pltpu.make_async_remote_copy(
            src_ref=total.at[dp], dst_ref=total.at[dp], send_sem=sum_s.at[n],
            recv_sem=sum_r.at[n], device_id={"dp": peer}, device_id_type=MESH)

    def wait_all(ref, sem):
        ref = ref.at[pl.ds(0, DP - 1)]
        pltpu.make_async_copy(ref, ref, sem).wait()

    for n, (chip, to) in enumerate(((z_dn, t_up), (z_up, t_dn), (z_far, t_far), (z, None))):
        if to is not None:
            proj_send(n, to).wait_recv()
        cols = pl.ds(pl.multiple_of(chip * CHIP, CHIP), CHIP)
        proj[:, cols] = split2(proj_in[chip])
    projected = proj[...]

    def p_slice(s):
        s = jnp.minimum(s, PSLICES - 1)
        cols = pl.ds(pl.multiple_of(s * PSLICE, PSLICE), PSLICE)
        return join2(dot(projected, h_buf[:, cols], (1, 0)))

    for peer in peers:
        p_part[peer] = p_slice(peer)
        scatter(p_part, p_in, peer, 0).start()
    p_in[dp] = p_slice(dp)
    pass_on(0)
    wait_all(p_in, sum_r.at[0])
    value = p_in[0]
    for s in range(1, DP):
        value = value + p_in[s]
    p_all[dp] = value
    for peer in peers:
        gather(p_all, peer, 1).start()
    pass_on(1)
    wait_all(p_all, sum_r.at[1])

    power = jnp.concatenate([p_all[s] for s in range(PSLICES)], axis=1)
    gram = lax.dot_general(
        power, power, (((1,), (1,)), ((), ())), precision=HIGH, preferred_element_type=F32)
    mapped_power = join2(dot(split2(power), ht_buf[...], (1, 0)))
    gram_schmidt(gram, coeff)
    mapped = split2(
        jnp.dot(coeff[...], mapped_power, precision=HIGH, preferred_element_type=F32))

    basis = jnp.dot(coeff[...], power, precision=HIGH, preferred_element_type=F32)
    p_ref[...] = basis
    p_turned_ref[...] = split2(basis).T
    for part in range(2):
        for way in range(2):
            onward(way, part).wait_recv()
            far_across(way, part).start()
    for n in range(2, 6):
        crossed(n)
    for part in range(2):
        for way in range(2):
            far_across(way, part).wait_recv()

    def q_slice(s):
        cols = pl.ds(pl.multiple_of(s * QSLICE, QSLICE), QSLICE)
        return join2(dot(mapped, g_buf[:, cols], (1, 0))).astype(BF16)

    for peer in peers:
        q_part[peer] = q_slice(peer)
        scatter(q_part, q_in, peer, 2).start()
    q_in[dp] = q_slice(dp)
    grad_tiles(0, FF // GRAD_TILE // 2)
    wait_all(q_in, sum_r.at[2])
    value = q_in[0].astype(F32)
    for s in range(1, DP):
        value = value + q_in[s].astype(F32)
    q_all[dp] = (value * (1.0 / DP)).astype(BF16)
    for peer in peers:
        gather(q_all, peer, 3).start()
    grad_tiles(FF // GRAD_TILE // 2, FF // GRAD_TILE)

    for way in range(2):
        for k in range(4):
            own(way, k).wait_send()
        for k in range(2):
            q_own(way, k).wait_send()
            onward(way, k).wait_send()
            far_across(way, k).wait_send()
        q_onward(way).wait_send()
    for n in range(6):
        across(n, tensor, 0).wait_send()
    for n in range(3):
        proj_send(n, t_up).wait_send()
        for line in range(2):
            pull(n, line).wait_send()
    for line in range(2):
        spread_wait(line, cross_s)
    wait_all(p_part, sum_s.at[0])
    wait_all(p_all, sum_s.at[1])
    wait_all(q_part, sum_s.at[2])
    wait_all(q_all, sum_s.at[3])
    wait_all(q_all, sum_r.at[3])


def error_kernel(
    grad_ref, p_ref, q_ref, p_turned_ref, p_out, q_out, error_out,
    q2, q_wide, error_buf, sem, factor_sem,
):
    factors = (
        pltpu.make_async_copy(p_ref, p_out, factor_sem.at[0]),
        pltpu.make_async_copy(q_wide, q_out, factor_sem.at[1]),
    )
    for s in range(DP):
        q2[:, s * QSLICE : (s + 1) * QSLICE] = jnp.concatenate([q_ref[s], q_ref[s]], axis=0)
    copies = []
    for m in range(FF // ERROR_TILE):
        rows = pl.ds(m * ERROR_TILE, ERROR_TILE)
        for c in range(0, D, ERROR_WIDTH):
            cols = pl.ds(c, ERROR_WIDTH)
            low_rank = dot(p_turned_ref[rows, :], q2[:, cols], (1, 0))
            error_buf[rows, cols] = (grad_ref[rows, cols] - low_rank).astype(BF16)
        copies.append(
            pltpu.make_async_copy(error_buf.at[rows], error_out.at[rows], sem.at[m]))
        copies[-1].start()
        if m == 0:
            for s in range(DP):
                q_wide[:, s * QSLICE : (s + 1) * QSLICE] = q_ref[s].astype(F32)
            for copy in factors:
                copy.start()
    for copy in copies:
        copy.wait()
    for copy in factors:
        copy.wait()


def on_device(gate_pre, up_pre, out_grad, q_start):
    hbm_in = [
        pltpu.with_memory_space_constraint(v, pltpu.HBM)
        for v in (gate_pre, up_pre, out_grad, q_start[0].T)
    ]
    any_space = pl.BlockSpec(memory_space=pl.ANY)
    vmem_space = pl.BlockSpec(memory_space=pltpu.VMEM)
    dma = pltpu.SemaphoreType.DMA
    grad, p_factor, q_sums, p_turned = pl.pallas_call(
        exchange_kernel,
        out_shape=(
            pltpu.VMEM((FF, D), F32),
            pltpu.VMEM((RANK, FF), F32),
            pltpu.VMEM((DP, RANK, QSLICE), BF16),
            pltpu.VMEM((FF, 2 * RANK), BF16),
        ),
        in_specs=[any_space] * 4,
        out_specs=(vmem_space,) * 4,
        scratch_shapes=[
            pltpu.VMEM((TOK, D), BF16),
            pltpu.VMEM((TOK, FF), BF16),
            pltpu.VMEM((TOK, FF), BF16),
            pltpu.VMEM((TOK, FF), BF16),
            pltpu.VMEM((FF, TOK), BF16),
            pltpu.VMEM((RANK, D), F32),
            pltpu.VMEM((4, RANK, RING), BF16),
            pltpu.VMEM((2, 4, 4, RANK, QSLICE), BF16),
            pltpu.VMEM((3, RANK, CHIP), F32),
            pltpu.VMEM((4, RANK, CHIP), F32),
            pltpu.VMEM((2 * RANK, TOK), BF16),
            pltpu.VMEM((RANK, RANK), F32),
            pltpu.VMEM((DP, RANK, PSLICE), F32),
            pltpu.VMEM((DP, RANK, PSLICE), F32),
            pltpu.VMEM((DP, RANK, PSLICE), F32),
            pltpu.VMEM((DP, RANK, QSLICE), BF16),
            pltpu.VMEM((DP, RANK, QSLICE), BF16),
            dma((5,)),
            dma((3, 2)), dma((3, 2)), dma((2,)), dma((2,)),
            dma((2, 2)), dma((2, 2)), dma((2,)), dma((2,)),
            dma((2, 4)), dma((2, 4)), dma((2, 2)), dma((2, 2)),
            dma((6,)), dma((6,)), dma((2, 2)), dma((2, 2)),
            dma((3,)), dma((3,)), dma((4,)), dma((4,)),
            pltpu.SemaphoreType.REGULAR((2,)),
        ],
        compiler_params=pltpu.CompilerParams(
            collective_id=0, has_side_effects=True, vmem_limit_bytes=VMEM_BYTES),
        name="exchange",
    )(*hbm_in)
    p_out, q_out, new_error = pl.pallas_call(
        error_kernel,
        out_shape=(
            jax.ShapeDtypeStruct((RANK, FF), F32),
            jax.ShapeDtypeStruct((RANK, D), F32),
            jax.ShapeDtypeStruct((FF, D), BF16),
        ),
        in_specs=[vmem_space] * 4,
        out_specs=(any_space,) * 3,
        scratch_shapes=[
            pltpu.VMEM((2 * RANK, D), BF16),
            pltpu.VMEM((RANK, D), F32),
            pltpu.VMEM((FF, D), BF16),
            dma((FF // ERROR_TILE,)),
            dma((2,)),
        ],
        compiler_params=pltpu.CompilerParams(vmem_limit_bytes=VMEM_BYTES),
        name="error",
    )(grad, p_factor, q_sums, p_turned)
    return (p_out.T, q_out.T[None], new_error[None])


def solution(mesh):
    placed = (
        P("dp", "tensor"),
        P("dp", "tensor"),
        P(("dp", "tensor"), None),
        P("tensor", None, None),
    )
    return jax.shard_map(
        on_device,
        mesh=mesh,
        in_specs=placed,
        out_specs=(P("tensor", None), P("tensor", None, None), P("dp", "tensor", None)),
        check_vma=False,
    )
```

```python
import functools

import jax
import jax.numpy as jnp
from jax import lax
from jax.experimental import pallas as pl
from jax.experimental.pallas import tpu as pltpu
from jax.sharding import PartitionSpec as P

EPSILON = 1e-06
HIGH = lax.Precision.HIGHEST
BF16 = jnp.bfloat16
F32 = jnp.float32
MESH = pl.DeviceIdType.MESH

TOK = 512
ROWS = 64
D = 4096
FF = 1792
RANK = 32
HALF = ROWS // 2
CHIP = 2 * ROWS
Q_HALF = 16
PART = HALF // 2
DP = 16
PSLICE = 128
PSLICES = FF // PSLICE
QSLICE = D // DP
LINE = 4 * QSLICE
RING = D - 2 * LINE
EARLY = 2
TILE = 256
WIDTH = 512
GRAD_TILE = 448
BLOCK = 4
ERROR_TILE = 128
ERROR_WIDTH = 256
VMEM_BYTES = 24 * 2**20


def dot(a, b, contract):
    return lax.dot_general(a, b, ((contract[:1], contract[1:]), ((), ())), preferred_element_type=F32)


def split2(x):
    high = x.astype(BF16)
    low = (x - high.astype(F32)).astype(BF16)
    return jnp.concatenate([high, low], axis=0)


def join2(x):
    return x[:RANK] + x[RANK:]


def gram_schmidt(gram, coeff_ref):
    rows = lax.broadcasted_iota(jnp.int32, (RANK, RANK), 0)
    cols = lax.broadcasted_iota(jnp.int32, (RANK, RANK), 1)
    y = gram
    u = jnp.where(rows == cols, 1.0, 0.0).astype(F32)
    base = 0

    def spread_row(m, r):
        return jnp.broadcast_to(m[r : r + 1, :], (8, RANK))

    def tall(m, n):
        return jnp.concatenate([m] * (n // 8), axis=0) if n > 8 else m

    for j in range(0, RANK, BLOCK):
        at = j - base
        left = RANK - base
        y_row = [spread_row(y, at + a) for a in range(BLOCK)]
        u_row = [spread_row(u, at + a) for a in range(BLOCK)]
        y_col = [jnp.broadcast_to(y[:, j + a : j + a + 1], (left, RANK)) for a in range(BLOCK)]
        pairs = [(a, c) for a in range(BLOCK) for c in range(a, BLOCK)]
        x = {
            (a, c): jnp.broadcast_to(
                jnp.sum(u_row[a] * y_row[c], axis=1, keepdims=True), (8, RANK))
            for a, c in pairs
        }
        v = {(a, c): spread_row(y_col[a], at + c) for a, c in pairs if c > a}
        inverse = []
        for a in range(BLOCK):
            norm = x[a, a]
            scale = lax.rsqrt(jnp.maximum(norm, 0.0) + EPSILON)
            inverse.append(scale * scale)
            coeff_ref[j + a : j + a + 1, :] = (u_row[a] * scale)[:1]
            f = {c: v[a, c] * inverse[a] for c in range(a + 1, BLOCK)}
            for c in range(a + 1, BLOCK):
                for d in range(c, BLOCK):
                    x[c, d] = x[c, d] - f[c] * x[a, d] - f[d] * (x[a, c] - norm * f[c])
                    if d > c:
                        v[c, d] = v[c, d] - f[c] * v[a, d]
                y_row[c] = y_row[c] - f[c] * y_row[a]
                u_row[c] = u_row[c] - f[c] * u_row[a]
                y_col[c] = y_col[c] - tall(f[c], left) * y_col[a]
        if j + BLOCK < RANK:
            for a in range(BLOCK):
                y = y - y_col[a] * tall(inverse[a] * y_row[a], left)
                u = u - y_col[a] * tall(inverse[a] * u_row[a], left)
            if (j + BLOCK) % 8 == 0:
                y = y[j + BLOCK - base :, :]
                u = u[j + BLOCK - base :, :]
                base = j + BLOCK


def exchange_kernel(
    gate_hbm, up_hbm, out_grad_hbm, q_hbm,
    grad_ref, p_ref, q_all, p_turned_ref,
    g_buf, gate_buf, up_buf, h_buf, ht_buf, q_buf, q_ring, q_cross, proj_out, proj_in, proj, coeff,
    p_part, p_in, p_all, q_part, q_in,
    local_sem, pull_s, pull_r, cross_s, cross_r, q_own_s, q_own_r, q_far_s, q_far_r, own_s, own_r, far_s, far_r,
    sib_s, sib_r, far_sib_s, far_sib_r, proj_s, proj_r, sum_s, sum_r, near_sem,
):
    dp = lax.axis_index("dp")
    tensor = lax.axis_index("tensor")
    z = tensor // 2
    core = lax.rem(tensor, 2)
    z_up, z_far, z_dn = lax.rem(z + 1, 4), lax.rem(z + 2, 4), lax.rem(z + 3, 4)
    t_up, t_far, t_dn = z_up * 2 + core, z_far * 2 + core, z_dn * 2 + core
    t_sib = z * 2 + 1 - core
    y = dp // 4
    x = lax.rem(dp, 4)
    hops = {
        (a, b): min(a, 4 - a) + min(b, 4 - b) for a in range(4) for b in range(4) if a or b
    }
    peer_at = {
        o: lax.rem(y + o[0], 4) * 4 + lax.rem(x + o[1], 4)
        for o in sorted(hops, key=lambda o: -hops[o])
    }
    peers = list(peer_at.values())
    near = [peer_at[o] for o in peer_at if hops[o] == 1]
    opposite = [peer_at[0, 2], peer_at[2, 0]]
    lines = ([peer_at[0, k] for k in (2, 1, 3)], [peer_at[k, 0] for k in (2, 1, 3)])

    def half_of(t, h):
        return pl.ds(pl.multiple_of(t * ROWS + h * HALF, HALF), HALF)

    def local_g(h):
        return pltpu.make_async_copy(
            out_grad_hbm.at[pl.ds(h * HALF, HALF), :], g_buf.at[half_of(tensor, h), :],
            local_sem.at[h])

    def local_in(k):
        src, dst = ((gate_hbm, gate_buf), (up_hbm, up_buf), (q_hbm, q_buf))[k]
        return pltpu.make_async_copy(src, dst, local_sem.at[2 + k])

    barrier = pltpu.get_barrier_semaphore()
    for t in (t_up, t_dn, t_far, t_sib):
        pl.semaphore_signal(barrier, inc=1, device_id={"tensor": t}, device_id_type=MESH)
    for peer in near:
        pl.semaphore_signal(barrier, inc=1, device_id={"dp": peer}, device_id_type=MESH)
    local_in(2).start()
    for h in range(2):
        local_g(h).start()
    for k in range(2):
        local_in(k).start()
    local_in(2).wait()
    q_ring[0] = q_buf[:, :RING].astype(BF16)
    for line in range(2):
        for k in range(4):
            col = RING + line * LINE + k * QSLICE
            q_cross[line, k, 0] = q_buf[:, col : col + QSLICE].astype(BF16)
    pl.semaphore_wait(barrier, 4 + len(near))

    def tell(n):
        for peer in (near, opposite)[n]:
            pl.semaphore_signal(
                near_sem.at[n], inc=1, device_id={"dp": peer}, device_id_type=MESH)

    def hear(n):
        pl.semaphore_wait(near_sem.at[n], (len(near), len(opposite))[n])

    def pull(n, line):
        to, place = ((t_up, 3), (t_dn, 1), (t_far, 2))[n]
        part = q_cross.at[line, (x, y)[line]]
        return pltpu.make_async_remote_copy(
            src_ref=part.at[0], dst_ref=part.at[place], send_sem=pull_s.at[n, line],
            recv_sem=pull_r.at[n, line], device_id={"tensor": to}, device_id_type=MESH)

    def spread(line, peer):
        ref = q_cross.at[line, (x, y)[line], pl.ds(1, 3)]
        return pltpu.make_async_remote_copy(
            src_ref=ref, dst_ref=ref, send_sem=cross_s.at[line], recv_sem=cross_r.at[line],
            device_id={"dp": peer}, device_id_type=MESH)

    def spread_wait(line, sem):
        ref = q_cross.at[line, pl.ds(0, 3), pl.ds(1, 3)]
        pltpu.make_async_copy(ref, ref, sem.at[line]).wait()

    def piece(t, h, to, send, recv):
        ref = g_buf.at[half_of(t, h), :]
        return pltpu.make_async_remote_copy(
            src_ref=ref, dst_ref=ref, send_sem=send, recv_sem=recv,
            device_id={"tensor": to}, device_id_type=MESH)

    pieces = ((0, PART, 0, D // 2), (0, PART, D // 2, D // 2), (PART, PART, 0, D), (0, HALF, 0, D))

    def own(way, k):
        h = 1 - way if k == 3 else way
        row, rows, col, cols = pieces[k]
        ref = g_buf.at[
            pl.ds(pl.multiple_of(tensor * ROWS + h * HALF + row, PART), rows), pl.ds(col, cols)]
        return pltpu.make_async_remote_copy(
            src_ref=ref, dst_ref=ref, send_sem=own_s.at[way, k], recv_sem=own_r.at[way, k],
            device_id={"tensor": (t_up, t_dn)[way]}, device_id_type=MESH)

    def part_of(t, h, part):
        return g_buf.at[pl.ds(pl.multiple_of(t * ROWS + h * HALF + part * PART, PART), PART), :]

    def onward(way, part):
        ref = part_of((t_dn, t_up)[way], way, part)
        return pltpu.make_async_remote_copy(
            src_ref=ref, dst_ref=ref, send_sem=far_s.at[way, part], recv_sem=far_r.at[way, part],
            device_id={"tensor": (t_up, t_dn)[way]}, device_id_type=MESH)

    def far_across(way, part):
        ref = part_of(t_far, way, part)
        return pltpu.make_async_remote_copy(
            src_ref=ref, dst_ref=ref, send_sem=far_sib_s.at[way, part],
            recv_sem=far_sib_r.at[way, part], device_id={"tensor": t_sib}, device_id_type=MESH)

    def across(n, t, h):
        return piece(t, h, t_sib, sib_s.at[n], sib_r.at[n])

    def q_piece(source, place, h, to, send, recv):
        rows = pl.ds(h * Q_HALF, Q_HALF)
        return pltpu.make_async_remote_copy(
            src_ref=q_ring.at[source, rows, :], dst_ref=q_ring.at[place, rows, :],
            send_sem=send, recv_sem=recv, device_id={"tensor": to}, device_id_type=MESH)

    def q_own(way, k):
        h = k if way == 0 else 1 - k
        return q_piece(
            0, (3, 1)[way], h, (t_up, t_dn)[way], q_own_s.at[way, k], q_own_r.at[way, k])

    def q_onward(way):
        return q_piece((3, 1)[way], 2, way, (t_up, t_dn)[way], q_far_s.at[way], q_far_r.at[way])

    for n in range(3):
        for line in range(2):
            pull(n, line).start()
    for k in range(2):
        for way in range(2):
            q_own(way, k).start()
    tell(0)
    for h in range(2):
        local_g(h).wait()
        across(h, tensor, h).start()
    hear(0)
    tell(1)
    for line in range(2):
        for n in range(3):
            pull(n, line).wait_recv()
        for peer in lines[line]:
            spread(line, peer).start()
    for way in range(2):
        q_own(way, 0).wait_recv()
        q_onward(way).start()
    for k in range(EARLY):
        for way in range(2):
            own(way, k).start()

    local_in(0).wait()
    local_in(1).wait()

    def make_hidden(i, carry):
        rows = pl.ds(pl.multiple_of(i * 64, 64), 64)
        v = gate_buf[rows, :].astype(F32)
        w = up_buf[rows, :].astype(F32)
        h_buf[rows, :] = ((0.5 * v) * (1.0 + jnp.tanh(0.5 * v)) * w).astype(BF16)
        return carry

    lax.fori_loop(0, TOK // 64, make_hidden, 0)

    def turn_hidden(i, carry):
        cols = pl.ds(pl.multiple_of(i * TILE, TILE), TILE)
        ht_buf[cols, :] = h_buf[:, cols].T
        return carry

    lax.fori_loop(0, FF // TILE, turn_hidden, 0)
    chip_rows = pl.ds(pl.multiple_of(z * CHIP, CHIP), CHIP)

    def proj_send(n, to):
        return pltpu.make_async_remote_copy(
            src_ref=proj_out.at[n], dst_ref=proj_in.at[z], send_sem=proj_s.at[n],
            recv_sem=proj_r.at[n], device_id={"tensor": to}, device_id_type=MESH)

    def crossed(n):
        across(n, tensor, 0).wait_recv()

    def pass_on(k):
        for way in range(2):
            if k == 0:
                own(way, 0).wait_recv()
                own(way, 1).wait_recv()
                onward(way, 0).start()
            else:
                own(way, 3).wait_recv()
                across(4 + way, (t_dn, t_up)[way], 1 - way).start()
        if k == 0:
            for way in range(2):
                own(way, 2).wait_recv()
                onward(way, 1).start()
                across(2 + way, (t_dn, t_up)[way], way).start()

    crossed(0)
    crossed(1)
    for way in range(2):
        q_own(way, 1).wait_recv()
        q_onward(way).wait_recv()
    results = dot(q_ring[...].reshape(4 * RANK, RING), g_buf[chip_rows, :RING], (1, 1))
    for line in range(2):
        spread_wait(line, cross_r)
        for k in range(4):
            col = RING + line * LINE + k * QSLICE
            results += dot(
                q_cross[line, k].reshape(4 * RANK, QSLICE), g_buf[chip_rows, col : col + QSLICE],
                (1, 1))
    proj_in[z] = results[:RANK]
    for n, (place, to) in enumerate(((1, t_up), (3, t_dn), (2, t_far))):
        proj_out[n] = results[place * RANK : (place + 1) * RANK]
    for n, to in ((2, t_far), (0, t_up), (1, t_dn)):
        proj_send(n, to).start()
    for k in range(EARLY, 4):
        for way in range(2):
            own(way, k).start()
    hear(1)

    def grad_tiles(first, last):
        def body(m, carry):
            rows = pl.ds(pl.multiple_of(m * GRAD_TILE, GRAD_TILE), GRAD_TILE)
            for c in range(0, D, WIDTH):
                cols = pl.ds(c, WIDTH)
                grad_ref[rows, cols] = dot(ht_buf[rows, :], g_buf[:, cols], (1, 0))
            return carry

        lax.fori_loop(first, last, body, 0)

    def scatter(part, landing, peer, n):
        return pltpu.make_async_remote_copy(
            src_ref=part.at[peer], dst_ref=landing.at[dp], send_sem=sum_s.at[n],
            recv_sem=sum_r.at[n], device_id={"dp": peer}, device_id_type=MESH)

    def gather(total, peer, n):
        return pltpu.make_async_remote_copy(
            src_ref=total.at[dp], dst_ref=total.at[dp], send_sem=sum_s.at[n],
            recv_sem=sum_r.at[n], device_id={"dp": peer}, device_id_type=MESH)

    def wait_all(ref, sem):
        ref = ref.at[pl.ds(0, DP - 1)]
        pltpu.make_async_copy(ref, ref, sem).wait()

    for n, (chip, to) in enumerate(((z_dn, t_up), (z_up, t_dn), (z_far, t_far), (z, None))):
        if to is not None:
            proj_send(n, to).wait_recv()
        cols = pl.ds(pl.multiple_of(chip * CHIP, CHIP), CHIP)
        proj[:, cols] = split2(proj_in[chip])
    projected = proj[...]

    def p_slice(s):
        s = jnp.minimum(s, PSLICES - 1)
        cols = pl.ds(pl.multiple_of(s * PSLICE, PSLICE), PSLICE)
        return join2(dot(projected, h_buf[:, cols], (1, 0)))

    for peer in peers:
        p_part[peer] = p_slice(peer).astype(BF16)
        scatter(p_part, p_in, peer, 0).start()
    p_in[dp] = p_slice(dp).astype(BF16)
    pass_on(0)
    wait_all(p_in, sum_r.at[0])
    value = p_in[0].astype(F32)
    for s in range(1, DP):
        value = value + p_in[s].astype(F32)
    p_all[dp] = value.astype(BF16)
    for peer in peers:
        gather(p_all, peer, 1).start()
    pass_on(1)
    wait_all(p_all, sum_r.at[1])

    power = jnp.concatenate([p_all[s] for s in range(PSLICES)], axis=1).astype(F32)
    gram = lax.dot_general(
        power, power, (((1,), (1,)), ((), ())), precision=HIGH, preferred_element_type=F32)
    mapped_power = join2(dot(split2(power), ht_buf[...], (1, 0)))
    gram_schmidt(gram, coeff)
    mapped = split2(
        jnp.dot(coeff[...], mapped_power, precision=HIGH, preferred_element_type=F32))

    basis = jnp.dot(coeff[...], power, precision=HIGH, preferred_element_type=F32)
    p_ref[...] = basis
    p_turned_ref[...] = split2(basis).T
    for part in range(2):
        for way in range(2):
            onward(way, part).wait_recv()
            far_across(way, part).start()
    for n in range(2, 6):
        crossed(n)
    for part in range(2):
        for way in range(2):
            far_across(way, part).wait_recv()

    def q_slice(s):
        cols = pl.ds(pl.multiple_of(s * QSLICE, QSLICE), QSLICE)
        return join2(dot(mapped, g_buf[:, cols], (1, 0))).astype(BF16)

    for peer in peers:
        q_part[peer] = q_slice(peer)
        scatter(q_part, q_in, peer, 2).start()
    q_in[dp] = q_slice(dp)
    grad_tiles(0, FF // GRAD_TILE // 2)
    wait_all(q_in, sum_r.at[2])
    value = q_in[0].astype(F32)
    for s in range(1, DP):
        value = value + q_in[s].astype(F32)
    q_all[dp] = (value * (1.0 / DP)).astype(BF16)
    for peer in peers:
        gather(q_all, peer, 3).start()
    grad_tiles(FF // GRAD_TILE // 2, FF // GRAD_TILE)

    for way in range(2):
        for k in range(4):
            own(way, k).wait_send()
        for k in range(2):
            q_own(way, k).wait_send()
            onward(way, k).wait_send()
            far_across(way, k).wait_send()
        q_onward(way).wait_send()
    for n in range(6):
        across(n, tensor, 0).wait_send()
    for n in range(3):
        proj_send(n, t_up).wait_send()
        for line in range(2):
            pull(n, line).wait_send()
    for line in range(2):
        spread_wait(line, cross_s)
    wait_all(p_part, sum_s.at[0])
    wait_all(p_all, sum_s.at[1])
    wait_all(q_part, sum_s.at[2])
    wait_all(q_all, sum_s.at[3])
    wait_all(q_all, sum_r.at[3])


def error_kernel(
    grad_ref, p_ref, q_ref, p_turned_ref, p_out, q_out, error_out,
    q2, q_wide, error_buf, sem, factor_sem,
):
    factors = (
        pltpu.make_async_copy(p_ref, p_out, factor_sem.at[0]),
        pltpu.make_async_copy(q_wide, q_out, factor_sem.at[1]),
    )
    for s in range(DP):
        q2[:, s * QSLICE : (s + 1) * QSLICE] = jnp.concatenate([q_ref[s], q_ref[s]], axis=0)
    copies = []
    for m in range(FF // ERROR_TILE):
        rows = pl.ds(m * ERROR_TILE, ERROR_TILE)
        for c in range(0, D, ERROR_WIDTH):
            cols = pl.ds(c, ERROR_WIDTH)
            low_rank = dot(p_turned_ref[rows, :], q2[:, cols], (1, 0))
            error_buf[rows, cols] = (grad_ref[rows, cols] - low_rank).astype(BF16)
        copies.append(
            pltpu.make_async_copy(error_buf.at[rows], error_out.at[rows], sem.at[m]))
        copies[-1].start()
        if m == 0:
            for s in range(DP):
                q_wide[:, s * QSLICE : (s + 1) * QSLICE] = q_ref[s].astype(F32)
            for copy in factors:
                copy.start()
    for copy in copies:
        copy.wait()
    for copy in factors:
        copy.wait()


def on_device(gate_pre, up_pre, out_grad, q_start):
    hbm_in = [
        pltpu.with_memory_space_constraint(v, pltpu.HBM)
        for v in (gate_pre, up_pre, out_grad, q_start[0].T)
    ]
    any_space = pl.BlockSpec(memory_space=pl.ANY)
    vmem_space = pl.BlockSpec(memory_space=pltpu.VMEM)
    dma = pltpu.SemaphoreType.DMA
    grad, p_factor, q_sums, p_turned = pl.pallas_call(
        exchange_kernel,
        out_shape=(
            pltpu.VMEM((FF, D), F32),
            pltpu.VMEM((RANK, FF), F32),
            pltpu.VMEM((DP, RANK, QSLICE), BF16),
            pltpu.VMEM((FF, 2 * RANK), BF16),
        ),
        in_specs=[any_space] * 4,
        out_specs=(vmem_space,) * 4,
        scratch_shapes=[
            pltpu.VMEM((TOK, D), BF16),
            pltpu.VMEM((TOK, FF), BF16),
            pltpu.VMEM((TOK, FF), BF16),
            pltpu.VMEM((TOK, FF), BF16),
            pltpu.VMEM((FF, TOK), BF16),
            pltpu.VMEM((RANK, D), F32),
            pltpu.VMEM((4, RANK, RING), BF16),
            pltpu.VMEM((2, 4, 4, RANK, QSLICE), BF16),
            pltpu.VMEM((3, RANK, CHIP), F32),
            pltpu.VMEM((4, RANK, CHIP), F32),
            pltpu.VMEM((2 * RANK, TOK), BF16),
            pltpu.VMEM((RANK, RANK), F32),
            pltpu.VMEM((DP, RANK, PSLICE), BF16),
            pltpu.VMEM((DP, RANK, PSLICE), BF16),
            pltpu.VMEM((DP, RANK, PSLICE), BF16),
            pltpu.VMEM((DP, RANK, QSLICE), BF16),
            pltpu.VMEM((DP, RANK, QSLICE), BF16),
            dma((5,)),
            dma((3, 2)), dma((3, 2)), dma((2,)), dma((2,)),
            dma((2, 2)), dma((2, 2)), dma((2,)), dma((2,)),
            dma((2, 4)), dma((2, 4)), dma((2, 2)), dma((2, 2)),
            dma((6,)), dma((6,)), dma((2, 2)), dma((2, 2)),
            dma((3,)), dma((3,)), dma((4,)), dma((4,)),
            pltpu.SemaphoreType.REGULAR((2,)),
        ],
        compiler_params=pltpu.CompilerParams(
            collective_id=0, has_side_effects=True, vmem_limit_bytes=VMEM_BYTES),
        name="exchange",
    )(*hbm_in)
    p_out, q_out, new_error = pl.pallas_call(
        error_kernel,
        out_shape=(
            jax.ShapeDtypeStruct((RANK, FF), F32),
            jax.ShapeDtypeStruct((RANK, D), F32),
            jax.ShapeDtypeStruct((FF, D), BF16),
        ),
        in_specs=[vmem_space] * 4,
        out_specs=(any_space,) * 3,
        scratch_shapes=[
            pltpu.VMEM((2 * RANK, D), BF16),
            pltpu.VMEM((RANK, D), F32),
            pltpu.VMEM((FF, D), BF16),
            dma((FF // ERROR_TILE,)),
            dma((2,)),
        ],
        compiler_params=pltpu.CompilerParams(vmem_limit_bytes=VMEM_BYTES),
        name="error",
    )(grad, p_factor, q_sums, p_turned)
    return (p_out.T, q_out.T[None], new_error[None])


def solution(mesh):
    placed = (
        P("dp", "tensor"),
        P("dp", "tensor"),
        P(("dp", "tensor"), None),
        P("tensor", None, None),
    )
    return jax.shard_map(
        on_device,
        mesh=mesh,
        in_specs=placed,
        out_specs=(P("tensor", None), P("tensor", None, None), P("dp", "tensor", None)),
        check_vma=False,
    )
```

```python
import functools

import jax
import jax.numpy as jnp
from jax import lax
from jax.experimental import pallas as pl
from jax.experimental.pallas import tpu as pltpu
from jax.sharding import PartitionSpec as P

EPSILON = 1e-06
HIGH = lax.Precision.HIGHEST
BF16 = jnp.bfloat16
F32 = jnp.float32
MESH = pl.DeviceIdType.MESH

TOK = 512
ROWS = 64
D = 4096
FF = 1792
RANK = 32
HALF = ROWS // 2
CHIP = 2 * ROWS
Q_HALF = 16
PART = HALF // 2
DP = 16
PSLICE = 128
PSLICES = FF // PSLICE
QSLICE = D // DP
LINE = 4 * QSLICE
RING = D - 2 * LINE
EARLY = 2
TILE = 256
WIDTH = 512
GRAD_TILE = 448
BLOCK = 4
ERROR_TILE = 128
ERROR_WIDTH = 256
VMEM_BYTES = 24 * 2**20


def dot(a, b, contract):
    return lax.dot_general(a, b, ((contract[:1], contract[1:]), ((), ())), preferred_element_type=F32)


def split2(x):
    high = x.astype(BF16)
    low = (x - high.astype(F32)).astype(BF16)
    return jnp.concatenate([high, low], axis=0)


def join2(x):
    return x[:RANK] + x[RANK:]


def gram_schmidt(gram, coeff_ref):
    rows = lax.broadcasted_iota(jnp.int32, (RANK, RANK), 0)
    cols = lax.broadcasted_iota(jnp.int32, (RANK, RANK), 1)
    y = gram
    u = jnp.where(rows == cols, 1.0, 0.0).astype(F32)
    base = 0

    def spread_row(m, r):
        return jnp.broadcast_to(m[r : r + 1, :], (8, RANK))

    def tall(m, n):
        return jnp.concatenate([m] * (n // 8), axis=0) if n > 8 else m

    for j in range(0, RANK, BLOCK):
        at = j - base
        left = RANK - base
        y_row = [spread_row(y, at + a) for a in range(BLOCK)]
        u_row = [spread_row(u, at + a) for a in range(BLOCK)]
        y_col = [jnp.broadcast_to(y[:, j + a : j + a + 1], (left, RANK)) for a in range(BLOCK)]
        pairs = [(a, c) for a in range(BLOCK) for c in range(a, BLOCK)]
        x = {
            (a, c): jnp.broadcast_to(
                jnp.sum(u_row[a] * y_row[c], axis=1, keepdims=True), (8, RANK))
            for a, c in pairs
        }
        v = {(a, c): spread_row(y_col[a], at + c) for a, c in pairs if c > a}
        inverse = []
        for a in range(BLOCK):
            norm = x[a, a]
            scale = lax.rsqrt(jnp.maximum(norm, 0.0) + EPSILON)
            inverse.append(scale * scale)
            coeff_ref[j + a : j + a + 1, :] = (u_row[a] * scale)[:1]
            f = {c: v[a, c] * inverse[a] for c in range(a + 1, BLOCK)}
            for c in range(a + 1, BLOCK):
                for d in range(c, BLOCK):
                    x[c, d] = x[c, d] - f[c] * x[a, d] - f[d] * (x[a, c] - norm * f[c])
                    if d > c:
                        v[c, d] = v[c, d] - f[c] * v[a, d]
                y_row[c] = y_row[c] - f[c] * y_row[a]
                u_row[c] = u_row[c] - f[c] * u_row[a]
                y_col[c] = y_col[c] - tall(f[c], left) * y_col[a]
        if j + BLOCK < RANK:
            for a in range(BLOCK):
                y = y - y_col[a] * tall(inverse[a] * y_row[a], left)
                u = u - y_col[a] * tall(inverse[a] * u_row[a], left)
            if (j + BLOCK) % 8 == 0:
                y = y[j + BLOCK - base :, :]
                u = u[j + BLOCK - base :, :]
                base = j + BLOCK


def exchange_kernel(
    gate_hbm, up_hbm, out_grad_hbm, q_hbm,
    grad_ref, p_ref, q_all, p_turned_ref,
    g_buf, gate_buf, up_buf, h_buf, ht_buf, q_buf, q_ring, q_cross, proj_out, proj_in, proj, coeff,
    p_part, p_in, p_all, q_part, q_in,
    local_sem, pull_s, pull_r, cross_s, cross_r, q_own_s, q_own_r, q_far_s, q_far_r, own_s, own_r, far_s, far_r,
    sib_s, sib_r, far_sib_s, far_sib_r, proj_s, proj_r, sum_s, sum_r, near_sem,
):
    dp = lax.axis_index("dp")
    tensor = lax.axis_index("tensor")
    z = tensor // 2
    core = lax.rem(tensor, 2)
    z_up, z_far, z_dn = lax.rem(z + 1, 4), lax.rem(z + 2, 4), lax.rem(z + 3, 4)
    t_up, t_far, t_dn = z_up * 2 + core, z_far * 2 + core, z_dn * 2 + core
    t_sib = z * 2 + 1 - core
    y = dp // 4
    x = lax.rem(dp, 4)
    hops = {
        (a, b): min(a, 4 - a) + min(b, 4 - b) for a in range(4) for b in range(4) if a or b
    }
    peer_at = {
        o: lax.rem(y + o[0], 4) * 4 + lax.rem(x + o[1], 4)
        for o in sorted(hops, key=lambda o: -hops[o])
    }
    peers = list(peer_at.values())
    near = [peer_at[o] for o in peer_at if hops[o] == 1]
    opposite = [peer_at[0, 2], peer_at[2, 0]]
    lines = ([peer_at[0, k] for k in (2, 1, 3)], [peer_at[k, 0] for k in (2, 1, 3)])

    def half_of(t, h):
        return pl.ds(pl.multiple_of(t * ROWS + h * HALF, HALF), HALF)

    def local_g(h):
        return pltpu.make_async_copy(
            out_grad_hbm.at[pl.ds(h * HALF, HALF), :], g_buf.at[half_of(tensor, h), :],
            local_sem.at[h])

    def local_in(k):
        src, dst = ((gate_hbm, gate_buf), (up_hbm, up_buf), (q_hbm, q_buf))[k]
        return pltpu.make_async_copy(src, dst, local_sem.at[2 + k])

    barrier = pltpu.get_barrier_semaphore()
    for t in (t_up, t_dn, t_far, t_sib):
        pl.semaphore_signal(barrier, inc=1, device_id={"tensor": t}, device_id_type=MESH)
    for peer in near:
        pl.semaphore_signal(barrier, inc=1, device_id={"dp": peer}, device_id_type=MESH)
    local_in(2).start()
    for h in range(2):
        local_g(h).start()
    for k in range(2):
        local_in(k).start()
    local_in(2).wait()
    q_ring[0] = q_buf[:, :RING].astype(BF16)
    for line in range(2):
        for k in range(4):
            col = RING + line * LINE + k * QSLICE
            q_cross[line, k, 0] = q_buf[:, col : col + QSLICE].astype(BF16)
    pl.semaphore_wait(barrier, 4 + len(near))

    def tell(n):
        for peer in (near, opposite)[n]:
            pl.semaphore_signal(
                near_sem.at[n], inc=1, device_id={"dp": peer}, device_id_type=MESH)

    def hear(n):
        pl.semaphore_wait(near_sem.at[n], (len(near), len(opposite))[n])

    def pull(n, line):
        to, place = ((t_up, 3), (t_dn, 1), (t_far, 2))[n]
        part = q_cross.at[line, (x, y)[line]]
        return pltpu.make_async_remote_copy(
            src_ref=part.at[0], dst_ref=part.at[place], send_sem=pull_s.at[n, line],
            recv_sem=pull_r.at[n, line], device_id={"tensor": to}, device_id_type=MESH)

    def spread(line, peer):
        ref = q_cross.at[line, (x, y)[line], pl.ds(1, 3)]
        return pltpu.make_async_remote_copy(
            src_ref=ref, dst_ref=ref, send_sem=cross_s.at[line], recv_sem=cross_r.at[line],
            device_id={"dp": peer}, device_id_type=MESH)

    def spread_wait(line, sem):
        ref = q_cross.at[line, pl.ds(0, 3), pl.ds(1, 3)]
        pltpu.make_async_copy(ref, ref, sem.at[line]).wait()

    def piece(t, h, to, send, recv):
        ref = g_buf.at[half_of(t, h), :]
        return pltpu.make_async_remote_copy(
            src_ref=ref, dst_ref=ref, send_sem=send, recv_sem=recv,
            device_id={"tensor": to}, device_id_type=MESH)

    pieces = ((0, PART, 0, D // 2), (0, PART, D // 2, D // 2), (PART, PART, 0, D), (0, HALF, 0, D))

    def own(way, k):
        h = 1 - way if k == 3 else way
        row, rows, col, cols = pieces[k]
        ref = g_buf.at[
            pl.ds(pl.multiple_of(tensor * ROWS + h * HALF + row, PART), rows), pl.ds(col, cols)]
        return pltpu.make_async_remote_copy(
            src_ref=ref, dst_ref=ref, send_sem=own_s.at[way, k], recv_sem=own_r.at[way, k],
            device_id={"tensor": (t_up, t_dn)[way]}, device_id_type=MESH)

    def part_of(t, h, part):
        return g_buf.at[pl.ds(pl.multiple_of(t * ROWS + h * HALF + part * PART, PART), PART), :]

    def onward(way, part):
        ref = part_of((t_dn, t_up)[way], way, part)
        return pltpu.make_async_remote_copy(
            src_ref=ref, dst_ref=ref, send_sem=far_s.at[way, part], recv_sem=far_r.at[way, part],
            device_id={"tensor": (t_up, t_dn)[way]}, device_id_type=MESH)

    def far_across(way, part):
        ref = part_of(t_far, way, part)
        return pltpu.make_async_remote_copy(
            src_ref=ref, dst_ref=ref, send_sem=far_sib_s.at[way, part],
            recv_sem=far_sib_r.at[way, part], device_id={"tensor": t_sib}, device_id_type=MESH)

    def across(n, t, h):
        return piece(t, h, t_sib, sib_s.at[n], sib_r.at[n])

    def q_piece(source, place, h, to, send, recv):
        rows = pl.ds(h * Q_HALF, Q_HALF)
        return pltpu.make_async_remote_copy(
            src_ref=q_ring.at[source, rows, :], dst_ref=q_ring.at[place, rows, :],
            send_sem=send, recv_sem=recv, device_id={"tensor": to}, device_id_type=MESH)

    def q_own(way, k):
        h = k if way == 0 else 1 - k
        return q_piece(
            0, (3, 1)[way], h, (t_up, t_dn)[way], q_own_s.at[way, k], q_own_r.at[way, k])

    def q_onward(way):
        return q_piece((3, 1)[way], 2, way, (t_up, t_dn)[way], q_far_s.at[way], q_far_r.at[way])

    for n in range(3):
        for line in range(2):
            pull(n, line).start()
    for k in range(2):
        for way in range(2):
            q_own(way, k).start()
    tell(0)
    for h in range(2):
        local_g(h).wait()
        across(h, tensor, h).start()
    hear(0)
    tell(1)
    for line in range(2):
        for n in range(3):
            pull(n, line).wait_recv()
        for peer in lines[line]:
            spread(line, peer).start()
    for way in range(2):
        q_own(way, 0).wait_recv()
        q_onward(way).start()
    for k in range(EARLY):
        for way in range(2):
            own(way, k).start()

    local_in(0).wait()
    local_in(1).wait()

    def make_hidden(i, carry):
        rows = pl.ds(pl.multiple_of(i * 64, 64), 64)
        v = gate_buf[rows, :].astype(F32)
        w = up_buf[rows, :].astype(F32)
        h_buf[rows, :] = ((0.5 * v) * (1.0 + jnp.tanh(0.5 * v)) * w).astype(BF16)
        return carry

    lax.fori_loop(0, TOK // 64, make_hidden, 0)

    def turn_hidden(i, carry):
        cols = pl.ds(pl.multiple_of(i * TILE, TILE), TILE)
        ht_buf[cols, :] = h_buf[:, cols].T
        return carry

    lax.fori_loop(0, FF // TILE, turn_hidden, 0)
    chip_rows = pl.ds(pl.multiple_of(z * CHIP, CHIP), CHIP)

    def proj_send(n, to):
        return pltpu.make_async_remote_copy(
            src_ref=proj_out.at[n], dst_ref=proj_in.at[z], send_sem=proj_s.at[n],
            recv_sem=proj_r.at[n], device_id={"tensor": to}, device_id_type=MESH)

    def crossed(n):
        across(n, tensor, 0).wait_recv()

    def pass_on(k):
        for way in range(2):
            if k == 0:
                own(way, 0).wait_recv()
                own(way, 1).wait_recv()
                onward(way, 0).start()
            else:
                own(way, 3).wait_recv()
                across(4 + way, (t_dn, t_up)[way], 1 - way).start()
        if k == 0:
            for way in range(2):
                own(way, 2).wait_recv()
                onward(way, 1).start()
                across(2 + way, (t_dn, t_up)[way], way).start()

    crossed(0)
    crossed(1)
    for way in range(2):
        q_own(way, 1).wait_recv()
        q_onward(way).wait_recv()
    results = dot(q_ring[...].reshape(4 * RANK, RING), g_buf[chip_rows, :RING], (1, 1))
    for line in range(2):
        spread_wait(line, cross_r)
        for k in range(4):
            col = RING + line * LINE + k * QSLICE
            results += dot(
                q_cross[line, k].reshape(4 * RANK, QSLICE), g_buf[chip_rows, col : col + QSLICE],
                (1, 1))
    proj_in[z] = results[:RANK]
    for n, (place, to) in enumerate(((1, t_up), (3, t_dn), (2, t_far))):
        proj_out[n] = results[place * RANK : (place + 1) * RANK]
    for n, to in ((2, t_far), (0, t_up), (1, t_dn)):
        proj_send(n, to).start()
    for k in range(EARLY, 4):
        for way in range(2):
            own(way, k).start()
    hear(1)

    def grad_tiles(first, last):
        def body(m, carry):
            rows = pl.ds(pl.multiple_of(m * GRAD_TILE, GRAD_TILE), GRAD_TILE)
            for c in range(0, D, WIDTH):
                cols = pl.ds(c, WIDTH)
                grad_ref[rows, cols] = dot(ht_buf[rows, :], g_buf[:, cols], (1, 0))
            return carry

        lax.fori_loop(first, last, body, 0)

    def scatter(part, landing, peer, n):
        return pltpu.make_async_remote_copy(
            src_ref=part.at[peer], dst_ref=landing.at[dp], send_sem=sum_s.at[n],
            recv_sem=sum_r.at[n], device_id={"dp": peer}, device_id_type=MESH)

    def gather(total, peer, n):
        return pltpu.make_async_remote_copy(
            src_ref=total.at[dp], dst_ref=total.at[dp], send_sem=sum_s.at[n],
            recv_sem=sum_r.at[n], device_id={"dp": peer}, device_id_type=MESH)

    def wait_all(ref, sem):
        ref = ref.at[pl.ds(0, DP - 1)]
        pltpu.make_async_copy(ref, ref, sem).wait()

    for n, (chip, to) in enumerate(((z_dn, t_up), (z_up, t_dn), (z_far, t_far), (z, None))):
        if to is not None:
            proj_send(n, to).wait_recv()
        cols = pl.ds(pl.multiple_of(chip * CHIP, CHIP), CHIP)
        proj[:, cols] = split2(proj_in[chip])
    projected = proj[...]

    def p_slice(s):
        s = jnp.minimum(s, PSLICES - 1)
        cols = pl.ds(pl.multiple_of(s * PSLICE, PSLICE), PSLICE)
        return join2(dot(projected, h_buf[:, cols], (1, 0)))

    for first in range(0, len(peers), 5):
        for peer in peers[first : first + 5]:
            p_part[peer] = p_slice(peer).astype(BF16)
        for peer in peers[first : first + 5]:
            scatter(p_part, p_in, peer, 0).start()
    p_in[dp] = p_slice(dp).astype(BF16)
    pass_on(0)
    wait_all(p_in, sum_r.at[0])
    value = p_in[0].astype(F32)
    for s in range(1, DP):
        value = value + p_in[s].astype(F32)
    p_all[dp] = value.astype(BF16)
    for peer in peers:
        gather(p_all, peer, 1).start()
    pass_on(1)
    wait_all(p_all, sum_r.at[1])

    power = jnp.concatenate([p_all[s] for s in range(PSLICES)], axis=1).astype(F32)
    gram = lax.dot_general(
        power, power, (((1,), (1,)), ((), ())), precision=HIGH, preferred_element_type=F32)
    mapped_power = join2(dot(split2(power), ht_buf[...], (1, 0)))
    gram_schmidt(gram, coeff)
    mapped = split2(
        jnp.dot(coeff[...], mapped_power, precision=HIGH, preferred_element_type=F32))

    basis = jnp.dot(coeff[...], power, precision=HIGH, preferred_element_type=F32)
    p_ref[...] = basis
    p_turned_ref[...] = split2(basis).T
    for part in range(2):
        for way in range(2):
            onward(way, part).wait_recv()
            far_across(way, part).start()
    for n in range(2, 6):
        crossed(n)
    for part in range(2):
        for way in range(2):
            far_across(way, part).wait_recv()

    def q_slice(s):
        cols = pl.ds(pl.multiple_of(s * QSLICE, QSLICE), QSLICE)
        return join2(dot(mapped, g_buf[:, cols], (1, 0))).astype(BF16)

    for first in range(0, len(peers), 5):
        for peer in peers[first : first + 5]:
            q_part[peer] = q_slice(peer)
        for peer in peers[first : first + 5]:
            scatter(q_part, q_in, peer, 2).start()
    q_in[dp] = q_slice(dp)
    grad_tiles(0, FF // GRAD_TILE // 2)
    wait_all(q_in, sum_r.at[2])
    value = q_in[0].astype(F32)
    for s in range(1, DP):
        value = value + q_in[s].astype(F32)
    q_all[dp] = (value * (1.0 / DP)).astype(BF16)
    for peer in peers:
        gather(q_all, peer, 3).start()
    grad_tiles(FF // GRAD_TILE // 2, FF // GRAD_TILE)

    for way in range(2):
        for k in range(4):
            own(way, k).wait_send()
        for k in range(2):
            q_own(way, k).wait_send()
            onward(way, k).wait_send()
            far_across(way, k).wait_send()
        q_onward(way).wait_send()
    for n in range(6):
        across(n, tensor, 0).wait_send()
    for n in range(3):
        proj_send(n, t_up).wait_send()
        for line in range(2):
            pull(n, line).wait_send()
    for line in range(2):
        spread_wait(line, cross_s)
    wait_all(p_part, sum_s.at[0])
    wait_all(p_all, sum_s.at[1])
    wait_all(q_part, sum_s.at[2])
    wait_all(q_all, sum_s.at[3])
    wait_all(q_all, sum_r.at[3])


def error_kernel(
    grad_ref, p_ref, q_ref, p_turned_ref, p_out, q_out, error_out,
    q2, q_wide, error_buf, sem, factor_sem,
):
    factors = (
        pltpu.make_async_copy(p_ref, p_out, factor_sem.at[0]),
        pltpu.make_async_copy(q_wide, q_out, factor_sem.at[1]),
    )
    for s in range(DP):
        q2[:, s * QSLICE : (s + 1) * QSLICE] = jnp.concatenate([q_ref[s], q_ref[s]], axis=0)
    copies = []
    for m in range(FF // ERROR_TILE):
        rows = pl.ds(m * ERROR_TILE, ERROR_TILE)
        for c in range(0, D, ERROR_WIDTH):
            cols = pl.ds(c, ERROR_WIDTH)
            low_rank = dot(p_turned_ref[rows, :], q2[:, cols], (1, 0))
            error_buf[rows, cols] = (grad_ref[rows, cols] - low_rank).astype(BF16)
        copies.append(
            pltpu.make_async_copy(error_buf.at[rows], error_out.at[rows], sem.at[m]))
        copies[-1].start()
        if m == 0:
            for s in range(DP):
                q_wide[:, s * QSLICE : (s + 1) * QSLICE] = q_ref[s].astype(F32)
            for copy in factors:
                copy.start()
    for copy in copies:
        copy.wait()
    for copy in factors:
        copy.wait()


def on_device(gate_pre, up_pre, out_grad, q_start):
    hbm_in = [
        pltpu.with_memory_space_constraint(v, pltpu.HBM)
        for v in (gate_pre, up_pre, out_grad, q_start[0].T)
    ]
    any_space = pl.BlockSpec(memory_space=pl.ANY)
    vmem_space = pl.BlockSpec(memory_space=pltpu.VMEM)
    dma = pltpu.SemaphoreType.DMA
    grad, p_factor, q_sums, p_turned = pl.pallas_call(
        exchange_kernel,
        out_shape=(
            pltpu.VMEM((FF, D), F32),
            pltpu.VMEM((RANK, FF), F32),
            pltpu.VMEM((DP, RANK, QSLICE), BF16),
            pltpu.VMEM((FF, 2 * RANK), BF16),
        ),
        in_specs=[any_space] * 4,
        out_specs=(vmem_space,) * 4,
        scratch_shapes=[
            pltpu.VMEM((TOK, D), BF16),
            pltpu.VMEM((TOK, FF), BF16),
            pltpu.VMEM((TOK, FF), BF16),
            pltpu.VMEM((TOK, FF), BF16),
            pltpu.VMEM((FF, TOK), BF16),
            pltpu.VMEM((RANK, D), F32),
            pltpu.VMEM((4, RANK, RING), BF16),
            pltpu.VMEM((2, 4, 4, RANK, QSLICE), BF16),
            pltpu.VMEM((3, RANK, CHIP), F32),
            pltpu.VMEM((4, RANK, CHIP), F32),
            pltpu.VMEM((2 * RANK, TOK), BF16),
            pltpu.VMEM((RANK, RANK), F32),
            pltpu.VMEM((DP, RANK, PSLICE), BF16),
            pltpu.VMEM((DP, RANK, PSLICE), BF16),
            pltpu.VMEM((DP, RANK, PSLICE), BF16),
            pltpu.VMEM((DP, RANK, QSLICE), BF16),
            pltpu.VMEM((DP, RANK, QSLICE), BF16),
            dma((5,)),
            dma((3, 2)), dma((3, 2)), dma((2,)), dma((2,)),
            dma((2, 2)), dma((2, 2)), dma((2,)), dma((2,)),
            dma((2, 4)), dma((2, 4)), dma((2, 2)), dma((2, 2)),
            dma((6,)), dma((6,)), dma((2, 2)), dma((2, 2)),
            dma((3,)), dma((3,)), dma((4,)), dma((4,)),
            pltpu.SemaphoreType.REGULAR((2,)),
        ],
        compiler_params=pltpu.CompilerParams(
            collective_id=0, has_side_effects=True, vmem_limit_bytes=VMEM_BYTES),
        name="exchange",
    )(*hbm_in)
    p_out, q_out, new_error = pl.pallas_call(
        error_kernel,
        out_shape=(
            jax.ShapeDtypeStruct((RANK, FF), F32),
            jax.ShapeDtypeStruct((RANK, D), F32),
            jax.ShapeDtypeStruct((FF, D), BF16),
        ),
        in_specs=[vmem_space] * 4,
        out_specs=(any_space,) * 3,
        scratch_shapes=[
            pltpu.VMEM((2 * RANK, D), BF16),
            pltpu.VMEM((RANK, D), F32),
            pltpu.VMEM((FF, D), BF16),
            dma((FF // ERROR_TILE,)),
            dma((2,)),
        ],
        compiler_params=pltpu.CompilerParams(vmem_limit_bytes=VMEM_BYTES),
        name="error",
    )(grad, p_factor, q_sums, p_turned)
    return (p_out.T, q_out.T[None], new_error[None])


def solution(mesh):
    placed = (
        P("dp", "tensor"),
        P("dp", "tensor"),
        P(("dp", "tensor"), None),
        P("tensor", None, None),
    )
    return jax.shard_map(
        on_device,
        mesh=mesh,
        in_specs=placed,
        out_specs=(P("tensor", None), P("tensor", None, None), P("dp", "tensor", None)),
        check_vma=False,
    )
```
